512 devices in a mesh: edge: 128 (over z, x, core), rep: 4 (over y).
Axes of the slice: x: 4, y: 4, z: 16, core: 2. Of those that a mesh axis runs over, the one named last changes fastest.
Arguments:
- node_feat: bfloat16 [4, 512, 3200], P('rep', 'edge'), may hold values from -6 to 6
- rotation: bfloat16 [4, 20480, 475], P('rep', 'edge'), may hold values from -4 to 4, as said below
- source_owner: int32 [4, 20480, 1], P('rep', 'edge'), may hold values from 0 to 127; in each aligned block of 160 rows (0 to 159, 160 to 319, ..., all dimensions but the last counted through in order) at most 2 rows name the same one
- source_row: int32 [4, 20480], P('rep', 'edge'), may hold values from 0 to 3
- target_row: int32 [4, 20480], P('rep', 'edge'), may hold values from 0 to 3
- live_count: int32 [4, 128], P('rep', 'edge'), may hold values from 1 to 160, 17920 in all within a row
- edge_bias: float32 [4, 20480, 8], P('rep', 'edge'), may hold values from -3 to 303
- w_m0: bfloat16 [1280, 640], P('edge'), may hold values from -0.15625 to 0.15625
- w_m1: bfloat16 [2, 1024, 512], P(None, 'edge'), may hold values from -0.125 to 0.125
- w_m2: bfloat16 [2, 768, 384], P(None, 'edge'), may hold values from -0.15625 to 0.15625
- w_alpha: bfloat16 [128, 8], replicated, may hold values from -1.5 to 1.5
- out_grad: float32 [4, 512, 3200], P('rep', 'edge'), may hold values from -6 to 6
Outputs:
- node_out: bfloat16 [4, 512, 3200], P('rep', 'edge')
- grad_nodes: float32 [4, 512, 3200], P('rep', 'edge')
- grad_w0: float32 [1280, 640], P('edge')
The draws below stay inside these ranges and needn't reach their ends.
Inputs may be any that keep to these rules, and one draw needn't show every extreme that they name: `source_owner`: within the edge rows of one device at most 2 have sources on one owner, and in some device exactly 2 do. `rotation`: an entry is zero unless its row and column belong to the same degree l.
All inputs are finite; a program needn't handle non-finite values. No bound on the sum of `live_count` on one device may be relied on, other than what follows from the above.
Results may differ from the reference program's by a relative error of at most 0.02.
Values may be sent and summed in bfloat16 or wider, within the bound.
No kernel may reach another device: no remote copies, remote signals or barrier semaphores. Data moves between devices by JAX's collectives and lax.ppermute only.
A program may use at most 128 MiB of HBM per device.

```python
import math
import jax
import jax.numpy as jnp
import numpy as np
from jax import lax

C = 128
HEADS = 8
LCOEF = 25
MCOEF = 19
NODE_DEV = 4
EDGE_DEV = 160
CAP = 2
NODES = 512
EDGES = 20480
N_EDGE = 128
N_REP = 4


def degree_tables():
    row_degree = np.array([0, 1, 2, 3, 4, 1, 2, 3, 4, 1, 2, 3, 4, 2, 3, 4, 2, 3, 4])
    col_degree = np.array([degree for degree in range(5) for _ in range(2 * degree + 1)])
    blocks = (row_degree[:, None] == col_degree[None, :]).astype(np.float32)
    scales = (1.0 / np.sqrt(2.0 * row_degree + 1.0)).astype(np.float32)
    return (jnp.asarray(blocks), jnp.asarray(scales))


def draw_rotation(key, part):
    blocks, scales = degree_tables()
    entries = jax.random.normal(jax.random.fold_in(key, 3), (N_REP, EDGES, MCOEF, LCOEF), jnp.float32)
    entries = jnp.clip(entries, -4.0, 4.0) * scales[:, None] * blocks
    return entries.reshape(N_REP, EDGES, MCOEF * LCOEF).astype(jnp.bfloat16)


def target_rows(key):
    return jax.random.randint(jax.random.fold_in(key, 7), (N_REP, EDGES), 0, NODE_DEV, dtype=jnp.int32)


def draw_target_row(key, part):
    return target_rows(key)


def draw_edge_bias(key, part):
    return jax.random.uniform(jax.random.fold_in(key, 9), (N_REP, EDGES, HEADS), jnp.float32, -3.0, 3.0)


def with_ends(values, stream_key, smallest, high):
    longest = values.shape.index(max(values.shape))
    spots = []
    for shift in (0, 1):
        where = [jax.random.randint(jax.random.fold_in(stream_key, axis), (), 0, length) for axis, length in enumerate(values.shape)]
        where[longest] = (where[longest] + shift) % values.shape[longest]
        spots.append(tuple(where))
    return values.at[spots[0]].set(smallest).at[spots[1]].set(high)


def block_scale(key, dims, split, low, high):
    def one(axis_at, shards_of):
        draws = jax.random.uniform(jax.random.fold_in(jax.random.fold_in(key, 6), axis_at), (shards_of,), jnp.float32, low / len(split), high / len(split))
        return jnp.repeat(jnp.exp(draws), dims[axis_at] // shards_of).reshape((-1,) + (1,) * (len(dims) - axis_at - 1))

    level = one(*split[0])
    for cut in split[1:]:
        level = level * one(*cut)
    return level


def split_up(count, total, limit, skew):
    portions = [(1 << 20) // math.isqrt(rank ** skew) + 1 for rank in range(2, count + 1)]
    rest, given = total - limit - (count - 1), [1] * (count - 1)
    while rest > 0:
        movable = [i for i in range(count - 1) if given[i] < limit]
        pool, budget = sum([portions[i] for i in movable]), rest
        for i in movable:
            addition = min(limit - given[i], max(1, budget * portions[i] // pool), rest)
            given[i] = given[i] + addition
            rest = rest - addition
    return np.array([limit] + given)


def ragged_sizes(stream_key, number_of, total, most, lean):
    if number_of == 2:
        one = jax.random.randint(stream_key, (), max(1, total - most), min(most, total - 1) + 1)
        return jnp.stack([one, total - one])
    sizes = jnp.asarray(split_up(number_of, total, most, lean), jnp.int32)
    pairs = (number_of - 1) // 2
    source_of, receiver = sizes[1:1 + 2 * pairs:2], sizes[2:2 + 2 * pairs:2]
    room = jnp.minimum(source_of - 1, most - receiver)
    moved = jax.random.randint(jax.random.fold_in(stream_key, 1), (pairs,), 0, 1 << 20) % (room + 1)
    sizes = sizes.at[1:1 + 2 * pairs:2].set(source_of - moved).at[2:2 + 2 * pairs:2].set(receiver + moved)
    return sizes[jax.random.permutation(jax.random.fold_in(stream_key, 2), number_of)]


def shared_out(own_key, own, number, rows, number_of, top, most, skew):
    ranking = jax.random.permutation(own_key, number_of)
    packed, common = shares(number_of, rows * top, most, skew, True), shares(number_of, rows * top, most, skew, False)
    places = jnp.arange(number_of)

    def named(tallies, offset_by):
        used = int((tallies > 0).sum())
        fixed = max(1, used // 4)
        moved = fixed + (places - fixed + offset_by * (used - fixed)) % max(1, number_of - fixed)
        return jnp.zeros((number_of,), jnp.int32).at[ranking[jnp.where(places < fixed, places, moved)]].set(jnp.asarray(tallies, jnp.int32))

    tallies = jnp.where(number % 4 == 0, named(packed, number // 4), named(common, number - number // 4 - 1))
    mixed = jax.random.permutation(jax.random.fold_in(own, 3), number_of)
    giver, taker = mixed[0:number_of // 2 * 2:2], mixed[1:number_of // 2 * 2:2]
    slack = jnp.minimum(tallies[giver] - 1, most - tallies[taker]) // 2
    slack = jnp.where((giver == ranking[0]) | (taker == ranking[0]) | (tallies[taker] == 0), 0, jnp.maximum(slack, 0))
    moved = jax.random.randint(jax.random.fold_in(own, 4), (number_of // 2,), 0, 1 << 20) % (slack + 1)
    tallies = tallies.at[giver].add(-moved).at[taker].add(moved)
    items = jnp.searchsorted(jnp.cumsum(tallies), jnp.arange(rows * top), side="right").astype(jnp.int32)
    table = items.reshape(top, rows).T
    table = table[jax.random.permutation(jax.random.fold_in(own, 1), rows)]
    offset_by = jax.random.randint(jax.random.fold_in(own, 2), (rows, 1), 0, top)
    return jnp.take_along_axis(table, (jnp.arange(top)[None, :] + offset_by) % top, axis=1)


def shares(amount, total, reach, lean, full):
    loads = [(1 << 20) // math.isqrt(rank ** lean) + 1 for rank in range(1, amount + 1)]
    largest = reach if full else min(reach, max(-(-total // amount), total * loads[0] // sum(loads)))
    least = 1 if total - largest >= amount - 1 else 0
    holding, rest = [largest] + [least] * (amount - 1), total - largest - least * (amount - 1)
    while rest > 0:
        movable = [i for i in range(1, amount) if holding[i] < largest] or [i for i in range(1, amount) if holding[i] < reach]
        pool, budget = sum([loads[i] for i in movable]), rest
        for i in movable:
            more = min(reach - holding[i], max(1, budget * loads[i] // pool), rest)
            holding[i] = holding[i] + more
            rest = rest - more
    return np.array(holding)


def scatter_about(stream_key, shape, scale, most, pieces=(), kind=jnp.bfloat16):
    result = scale * jax.random.normal(stream_key, shape, jnp.float32)
    if pieces:
        result = result * block_scale(stream_key, shape, pieces, -0.22, 0.18)
    return jnp.clip(result, -most, most).astype(kind)


def setup_inputs(seed: int = 0) -> dict:
    keys = jax.random.split(jax.random.key(seed), 13)
    node_feat = scatter_about(keys[0], (N_REP, NODES, LCOEF * C), 1.0, 6.0, ((0, 4), (1, 128)))
    rotation = draw_rotation(jax.random.fold_in(keys[12], 71), 0)
    source_owner_keys = jax.random.split(jax.random.fold_in(keys[2], 1), N_REP * EDGES // EDGE_DEV)
    source_owner_turns = jax.random.permutation(jax.random.fold_in(keys[2], 3), N_REP * EDGES // EDGE_DEV)
    source_owner = jax.vmap(lambda own, number: shared_out(jax.random.fold_in(keys[2], 2), own, number, EDGE_DEV, N_EDGE, 1, CAP, 2))(source_owner_keys, source_owner_turns).reshape((N_REP, EDGES, 1))
    source_row = with_ends(jax.random.randint(keys[3], (N_REP, EDGES), 0, NODE_DEV), jax.random.fold_in(keys[3], 1), 0, NODE_DEV - 1).astype(jnp.int32)
    target_row = draw_target_row(jax.random.fold_in(keys[12], 71), 0)
    live_count = jax.vmap(lambda own: ragged_sizes(own, N_EDGE, N_EDGE * EDGE_DEV * 7 // 8, EDGE_DEV, 2))(jax.random.split(keys[5], N_REP)).reshape((N_REP, N_EDGE)).astype(jnp.int32)
    edge_bias = draw_edge_bias(jax.random.fold_in(keys[12], 71), 0)
    w_m0 = scatter_about(keys[7], (10 * C, 5 * C), (10 * C) ** -0.5, 0.15625, ((0, 128),))
    w_m1 = scatter_about(keys[8], (2, 8 * C, 4 * C), (16 * C) ** -0.5, 0.125, ((1, 128),))
    w_m2 = scatter_about(keys[9], (2, 6 * C, 3 * C), (12 * C) ** -0.5, 0.15625, ((1, 128),))
    w_alpha = scatter_about(keys[10], (C, HEADS), 0.25, 1.5)
    out_grad = scatter_about(keys[11], (N_REP, NODES, LCOEF * C), 1.0, 6.0, ((0, 4), (1, 128)), jnp.float32)
    return {"node_feat": node_feat, "rotation": rotation, "source_owner": source_owner, "source_row": source_row, "target_row": target_row, "live_count": live_count, "edge_bias": edge_bias, "w_m0": w_m0, "w_m1": w_m1, "w_m2": w_m2, "w_alpha": w_alpha, "out_grad": out_grad}


def layer_sums(message_in, w_zero, w_one, w_two, w_alpha, edge_bias, rotors, targets, is_live, row_count):
    edge_count = message_in.shape[0]
    full_width = message_in.shape[2]
    channels = full_width // 2
    heads = w_alpha.shape[1]

    def flat(first, last):
        return message_in[:, first:last, :].reshape(edge_count, (last - first) * full_width)

    def pair(plus, minus, weights):
        real_part = jnp.dot(plus, weights[0], preferred_element_type=jnp.float32) - jnp.dot(minus, weights[1], preferred_element_type=jnp.float32)
        imag_part = jnp.dot(minus, weights[0], preferred_element_type=jnp.float32) + jnp.dot(plus, weights[1], preferred_element_type=jnp.float32)
        return (real_part, imag_part)
    z_zero = jnp.dot(flat(0, 5), w_zero, preferred_element_type=jnp.float32)
    z_plus1, z_minus1 = pair(flat(5, 9), flat(9, 13), w_one)
    z_plus2, z_minus2 = pair(flat(13, 16), flat(16, 19), w_two)
    z_all = jnp.concatenate([z_zero, z_plus1, z_minus1, z_plus2, z_minus2], axis=1).reshape(edge_count, MCOEF, channels)
    values = z_all.astype(jnp.bfloat16)
    scalars = jax.nn.silu(z_all[:, 0, :]).astype(jnp.bfloat16)
    logits = edge_bias + jnp.dot(scalars, w_alpha, preferred_element_type=jnp.float32)
    member = (jnp.arange(row_count, dtype=jnp.int32)[:, None] == targets[None, :]) & is_live[None, :]
    highest = lax.optimization_barrier(jnp.max(jnp.where(member[:, :, None], logits[None, :, :], jnp.float32(-1e+30)), axis=1))
    highest = lax.stop_gradient(highest)
    shifted = jnp.where(is_live[:, None], logits - highest[targets], jnp.float32(0.0))
    expo = jnp.where(is_live[:, None], jnp.exp(shifted), jnp.float32(0.0))
    member_f = member.astype(jnp.float32)
    totals = jnp.dot(member_f, expo, precision=lax.Precision.HIGHEST)
    denom = jnp.where(is_live[:, None], totals[targets], jnp.float32(1.0))
    attn = expo / denom
    back = jnp.einsum('erk,erc->ekc', rotors.astype(jnp.float32), values.astype(jnp.float32))
    scale = jnp.repeat(attn, channels // heads, axis=1)
    weighted = (back * scale[:, None, :]).reshape(edge_count, LCOEF * channels)
    return jnp.dot(member_f, weighted, precision=lax.Precision.HIGHEST)

def reference(node_feat, rotation, source_owner, source_row, target_row, live_count, edge_bias, w_m0, w_m1, w_m2, w_alpha, out_grad):
    full_width = LCOEF * C
    outputs = []
    gradients = []
    weight_total = jnp.zeros(w_m0.shape, jnp.float32)
    for replica in range(N_REP):
        features = node_feat[replica]

        def device_step(carry, device):
            node_grad, weight_grad = carry
            start = (device * EDGE_DEV).astype(jnp.int32)

            def cut(array):
                return lax.dynamic_slice_in_dim(array, start, EDGE_DEV, 0)
            rotors = cut(rotation[replica]).reshape(EDGE_DEV, MCOEF, LCOEF)
            sources = (cut(source_owner[replica, :, 0]) * NODE_DEV + cut(source_row[replica])).astype(jnp.int32)
            targets = cut(target_row[replica]).astype(jnp.int32)
            target_ids = (device * NODE_DEV + targets).astype(jnp.int32)
            is_live = jnp.arange(EDGE_DEV, dtype=jnp.int32) < live_count[replica, device]
            biases = cut(edge_bias[replica])
            rot_f = rotors.astype(jnp.float32)
            src_feat = features[sources].reshape(EDGE_DEV, LCOEF, C).astype(jnp.float32)
            dst_feat = features[target_ids].reshape(EDGE_DEV, LCOEF, C).astype(jnp.float32)
            rotated_src = jnp.einsum('erk,ekc->erc', rot_f, src_feat).astype(jnp.bfloat16)
            rotated_dst = jnp.einsum('erk,ekc->erc', rot_f, dst_feat).astype(jnp.bfloat16)
            message_in = jnp.concatenate([rotated_src, rotated_dst], axis=2)

            def local_sums(message, weight):
                return layer_sums(message, weight, w_m1, w_m2, w_alpha, biases, rotors, targets, is_live, NODE_DEV)
            node_sums, pullback = jax.vjp(local_sums, message_in, w_m0)
            cotangent = lax.dynamic_slice_in_dim(out_grad[replica], (device * NODE_DEV).astype(jnp.int32), NODE_DEV, 0)
            grad_msg, grad_weight = pullback(cotangent)
            src_terms = jnp.einsum('erk,erc->ekc', rot_f, grad_msg[:, :, :C].astype(jnp.float32)).astype(jnp.bfloat16)
            src_terms = lax.optimization_barrier(src_terms).astype(jnp.float32).reshape(EDGE_DEV, full_width)
            dst_terms = jnp.einsum('erk,erc->ekc', rot_f, grad_msg[:, :, C:].astype(jnp.float32)).reshape(EDGE_DEV, full_width)
            node_grad = node_grad.at[sources].add(src_terms).at[target_ids].add(dst_terms)
            weight_grad = weight_grad + grad_weight.astype(jnp.float32)
            return ((node_grad, weight_grad), node_sums.astype(jnp.bfloat16))
        start_grad = jnp.zeros((NODES, full_width), jnp.float32)
        (node_grad, weight_total), blocks = lax.scan(device_step, (start_grad, weight_total), jnp.arange(N_EDGE, dtype=jnp.int32))
        outputs.append(blocks.reshape(NODES, full_width))
        gradients.append(node_grad)
    return (jnp.stack(outputs), jnp.stack(gradients), weight_total)
```

```python
import jax
import jax.numpy as jnp
from jax import lax
from jax.experimental import pallas as pl
from jax.experimental.pallas import tpu as pltpu
from jax.sharding import PartitionSpec as P

LCOEF = 25
MCOEF = 19
CH = 128
HEADS = 8
EDGES = 160
BLOCK = 16
NZ, NX = 16, 4
FULL = LCOEF * CH
ROWS_OF = {0: (0,), 1: (1, 5, 9), 2: (2, 6, 10, 13, 16), 3: (3, 7, 11, 14, 17), 4: (4, 8, 12, 15, 18)}
NEAR = (0, 1, 2, -1)
W_SPLIT = 800 + 3 * 128
VMEM_LIMIT = 56 * 2**20
F32, BF16 = jnp.float32, jnp.bfloat16


def where_to(i, dz, dx, dc):
    z, x, c = i // 8, (i // 2) % 4, i % 2
    sign = 1 - 2 * c
    return ((z + sign * dz) % NZ) * 8 + ((x + dx) % NX) * 2 + (c + dc) % 2


def pull(a, dz=0, dx=0, dc=0):
    return lax.ppermute(a, "edge", [(where_to(i, dz, dx, dc), i) for i in range(128)])


def push(a, dz=0, dx=0, dc=0):
    return lax.ppermute(a, "edge", [(i, where_to(i, dz, dx, dc)) for i in range(128)])


def block_place(owner, me):
    sign = 1 - 2 * (owner % 2)
    jz = (sign * (owner // 8 - me // 8) + 1) % NZ
    xr = ((owner // 2) % 4 - (me // 2) % 4) % NX
    cr = (owner % 2 + me % 2) % 2
    near = (jz % 4 + 3) % 4
    return cr * 64 + xr * 16 + near * 4 + jz // 4


def block_owner(place, me):
    cr, xr, near, far = place // 64, (place // 16) % 4, (place // 4) % 4, place % 4
    sign = 1 - 2 * ((me + cr) % 2)
    offset = (near + 1) % 4 - 1
    z = (me // 8 + sign * (4 * far + offset)) % NZ
    x = ((me // 2) % 4 + xr) % NX
    return z * 8 + x * 2 + (me % 2 + cr) % 2


def x_and_core(block, split):
    right, left = pull(block, dx=1), pull(block, dx=3)
    upper, lower = pull(right[:split], dx=1), pull(left[split:], dx=3)
    mine = (block, right, upper, lower, left)
    return mine + tuple(pull(a, dc=1) for a in mine)


def scatter_sum(pieces, split, near_rows, far_rows):
    def add(a, *more):
        total = a.astype(F32)
        for m in more:
            total = total + m.astype(F32)
        return total

    a = [add(pieces[x], push(pieces[4 + x], dc=1)).astype(BF16) for x in range(4)]
    up, down = push(a[2][:split], dx=1), push(a[2][split:], dx=3)
    right = jnp.concatenate([add(a[1][:split], up).astype(BF16), a[1][split:]], axis=0)
    left = jnp.concatenate([a[3][:split], add(a[3][split:], down).astype(BF16)], axis=0)
    total = add(a[0], push(right, dx=1), push(left, dx=3)).astype(BF16)
    parts = [total[n * near_rows : (n + 1) * near_rows] for n in range(4)]
    total = add(parts[0], *(push(parts[n], dz=NEAR[n]) for n in (1, 2, 3))).astype(BF16)
    parts = [total[n * far_rows : (n + 1) * far_rows] for n in range(4)]
    return add(parts[0], *(push(parts[n], dz=4 * n) for n in (1, 2, 3)))


def hot(index, shape, axis):
    return jnp.where(index == lax.broadcasted_iota(jnp.int32, shape, axis), F32(1), F32(0)).astype(BF16)


def mm(a, b):
    return jnp.dot(a, b, preferred_element_type=F32)


def mm_nt(a, b):
    return lax.dot_general(a, b, (((1,), (1,)), ((), ())), preferred_element_type=F32)


def frame_slot(row):
    if row < 5:
        return 0, 0, row
    if row < 13:
        return 1, ((row - 5) // 4) * EDGES, (row - 5) % 4
    return 2, ((row - 13) // 3) * EDGES, (row - 13) % 3


def rotate_kernel(*refs):
    pieces = refs[:10]
    rot, place, target, local, inv0, inv1, inv2 = refs[10:17]
    m0, m1, m2, turned_grad = refs[17:21]
    feats, srcf, dstf, gradf, n0, n1, n2 = refs[21:]
    for core in range(2):
        row = core * 256
        for piece in pieces[core * 5 : core * 5 + 5]:
            feats[row : row + piece.shape[0], :] = piece[...]
            row += piece.shape[0]
    source_hot = hot(place[...], (EDGES, 512), 1)
    t = target[...]
    lanes = lax.broadcasted_iota(jnp.int32, (EDGES, 16), 1)
    feat_hot = jnp.where(lanes == t, F32(1), F32(0)).astype(BF16)
    grad_hot = jnp.where((lanes == t + 4) | (lanes == t + 8), F32(1), F32(0)).astype(BF16)
    for first in range(0, FULL, 640):
        cut = slice(first, first + 640)
        srcf[:, cut] = mm(source_hot, feats[:, cut]).astype(BF16)
        dstf[:, cut] = mm(feat_hot, local[:, cut]).astype(BF16)
        gradf[:, cut] = mm(grad_hot, local[:, cut])

    stacked = (n0, n1, n2)

    def turn(step, carry):
        e0 = pl.multiple_of(step * BLOCK, BLOCK)
        rows_here = pl.ds(e0, BLOCK)
        rotors = rot[rows_here, :].astype(F32)
        for degree, rows in ROWS_OF.items():
            sums = [None] * len(rows)
            for col in range(degree * degree, (degree + 1) ** 2):
                cut = slice(col * CH, (col + 1) * CH)
                s, d, g = srcf[rows_here, cut].astype(F32), dstf[rows_here, cut].astype(F32), gradf[rows_here, cut]
                for n, row in enumerate(rows):
                    r = jnp.broadcast_to(rotors[:, row * LCOEF + col : row * LCOEF + col + 1], (BLOCK, CH))
                    terms = (r * s, r * d, r * g)
                    sums[n] = terms if sums[n] is None else tuple(a + b for a, b in zip(sums[n], terms))
            for n, row in enumerate(rows):
                array, base, column = frame_slot(row)
                out = stacked[array]
                out_rows = pl.ds(pl.multiple_of(base + e0, BLOCK), BLOCK)
                out[out_rows, column * 256 : column * 256 + CH] = sums[n][0].astype(BF16)
                out[out_rows, column * 256 + CH : column * 256 + 256] = sums[n][1].astype(BF16)
                turned_grad[rows_here, row * CH : (row + 1) * CH] = sums[n][2]
        return carry

    lax.fori_loop(0, EDGES // BLOCK, turn, 0)
    for natural, ordered, inverse in ((n0, m0, inv0), (n1, m1, inv1), (n2, m2, inv2)):
        depth = natural.shape[1]
        for first in range(0, depth, 256):
            cut = slice(first, first + 256)
            ordered[:, cut] = mm(natural[...], hot(inverse[:, cut], (depth, 256), 0)).astype(BF16)


def layer_kernel(*refs):
    pieces = refs[:10]
    m0, m1, m2, turned_grad, rot, bias, target, live_ref, alpha_ref, place, pos0, pos1, pos2 = refs[10:23]
    terms_out = refs[23:31]
    w0_out = refs[31:39]
    scaled_out, grad_dst = refs[39:41]
    w0, w1, w2, values, d0, d1, d2, p0, p1, p2, g0, g1, g2, src_terms = refs[41:]

    def place_rows(piece, core, x, begin, end):
        k = core * 4 + x
        at = 0
        for out, units, rows in ((w0, 5, 160), (w1, 8, 128), (w2, 6, 96)):
            for u in range(units):
                if begin <= at < end:
                    out[k * rows : (k + 1) * rows, u * CH : (u + 1) * CH] = piece[at - begin : at - begin + rows, :]
                at += rows

    for core in range(2):
        own, right, upper, lower, left = pieces[core * 5 : core * 5 + 5]
        place_rows(own, core, 0, 0, 2400)
        place_rows(right, core, 1, 0, 2400)
        place_rows(upper, core, 2, 0, W_SPLIT)
        place_rows(lower, core, 2, W_SPLIT, 2400)
        place_rows(left, core, 3, 0, 2400)

    z0 = mm(m0[...], w0[...])
    for row in range(5):
        values[:, row * CH : (row + 1) * CH] = z0[:, row * CH : (row + 1) * CH].astype(BF16)
    z1 = mm(m1[...], w1[...])
    values[:, 5 * CH : 9 * CH] = (z1[:EDGES, :512] - z1[EDGES:, 512:]).astype(BF16)
    values[:, 9 * CH : 13 * CH] = (z1[EDGES:, :512] + z1[:EDGES, 512:]).astype(BF16)
    z2 = mm(m2[...], w2[...])
    values[:, 13 * CH : 16 * CH] = (z2[:EDGES, :384] - z2[EDGES:, 384:]).astype(BF16)
    values[:, 16 * CH : 19 * CH] = (z2[EDGES:, :384] + z2[:EDGES, 384:]).astype(BF16)

    v = z0[:, :CH]
    sigma = 1.0 / (1.0 + jnp.exp(-v))
    alpha = alpha_ref[...]
    logits = bias[...] + mm((v * sigma).astype(BF16), alpha)
    live = live_ref[...] > 0
    t = target[...]
    members = [live & (t == n) for n in range(4)]

    def over_targets(array, empty, reduce):
        result = jnp.zeros((EDGES, HEADS), F32)
        for member in members:
            one = reduce(jnp.where(member, array, F32(empty)), axis=0, keepdims=True)
            result = jnp.where(member, one, result)
        return result

    top = over_targets(logits, -1e30, jnp.max)
    expo = jnp.where(live, jnp.exp(jnp.where(live, logits - top, F32(0))), F32(0))
    denom = jnp.where(live, over_targets(expo, 0.0, jnp.sum), F32(1))
    attn = expo / denom
    head_of = (
        lax.broadcasted_iota(jnp.int32, (HEADS, CH), 1) // (CH // HEADS)
        == lax.broadcasted_iota(jnp.int32, (HEADS, CH), 0)
    )
    spread = jnp.where(head_of, F32(1), F32(0))
    scale = jnp.dot(attn, spread, precision=lax.Precision.HIGHEST, preferred_element_type=F32)
    dscale = jnp.zeros((EDGES, CH), F32)
    for row in range(MCOEF):
        cut = slice(row * CH, (row + 1) * CH)
        value = values[:, cut].astype(F32)
        dscale = dscale + turned_grad[:, cut] * value
        scaled_out[:, cut] = (scale * value).astype(BF16)
    dattn = lax.dot_general(
        dscale, spread, (((1,), (1,)), ((), ())), precision=lax.Precision.HIGHEST, preferred_element_type=F32
    )
    dlogits = attn * (dattn - over_targets(attn * dattn, 0.0, jnp.sum))
    dscalars = lax.dot_general(
        dlogits, alpha.astype(F32), (((1,), (1,)), ((), ())), precision=lax.Precision.HIGHEST,
        preferred_element_type=F32,
    ).astype(BF16).astype(F32)
    dv = dscalars * (sigma * (1.0 + v * (1.0 - sigma)))
    for row in range(MCOEF):
        cut = slice(row * CH, (row + 1) * CH)
        dvalue = (scale * turned_grad[:, cut]).astype(BF16)
        if row == 0:
            dvalue = (dvalue.astype(F32) + dv).astype(BF16)
        if row < 5:
            d0[:, cut] = dvalue
            continue
        out, width, column, plus = (d1, 512, (row - 5) % 4, row < 9) if row < 13 else (d2, 384, (row - 13) % 3, row < 16)
        a, b = column * CH, width + column * CH
        if plus:
            out[:EDGES, a : a + CH] = dvalue
            out[EDGES:, b : b + CH] = -dvalue
        else:
            out[EDGES:, a : a + CH] = dvalue
            out[:EDGES, b : b + CH] = dvalue
    dw = lax.dot_general(m0[...], d0[...], (((0,), (0,)), ((), ())), preferred_element_type=F32)
    for k in range(8):
        w0_out[k][...] = dw[k * 160 : (k + 1) * 160].astype(BF16)
    for d, w, p, g, pos in ((d0, w0, p0, g0, pos0), (d1, w1, p1, g1, pos1), (d2, w2, p2, g2, pos2)):
        depth = w.shape[0]
        p[...] = mm_nt(d[...], w[...]).astype(BF16)
        for first in range(0, depth, 256):
            cut = slice(first, first + 256)
            g[:, cut] = mm(p[...], hot(pos[:, cut], (depth, 256), 0)).astype(BF16)
    stacked = (g0, g1, g2)
    for row in range(MCOEF):
        array, base, column = frame_slot(row)
        grad_dst[:, row * CH : (row + 1) * CH] = stacked[array][base : base + EDGES, column * 256 + CH : column * 256 + 256]

    def turn(step, carry):
        e0 = pl.multiple_of(step * BLOCK, BLOCK)
        rows_here = pl.ds(e0, BLOCK)
        rotors = rot[rows_here, :].astype(F32)
        for degree, rows in ROWS_OF.items():
            first = degree * degree
            sums = [None] * (2 * degree + 1)
            for row in rows:
                array, base, column = frame_slot(row)
                s = stacked[array][pl.ds(pl.multiple_of(base + e0, BLOCK), BLOCK), column * 256 : column * 256 + CH]
                s = s.astype(F32)
                for n in range(2 * degree + 1):
                    at = row * LCOEF + first + n
                    term = jnp.broadcast_to(rotors[:, at : at + 1], (BLOCK, CH)) * s
                    sums[n] = term if sums[n] is None else sums[n] + term
            for n in range(2 * degree + 1):
                src_terms[rows_here, (first + n) * CH : (first + n + 1) * CH] = sums[n].astype(BF16)
        return carry

    lax.fori_loop(0, EDGES // BLOCK, turn, 0)
    for k in range(8):
        chosen = hot(place[...] - k * 64, (64, EDGES), 0)
        for first in range(0, FULL, 640):
            cut = slice(first, first + 640)
            terms_out[k][:, cut] = mm(chosen, src_terms[:, cut]).astype(BF16)


def nodes_kernel(rot, scaled, grad_dst, target, node_out, grad_local, back, terms):
    def turn(step, carry):
        e0 = pl.multiple_of(step * BLOCK, BLOCK)
        rows_here = pl.ds(e0, BLOCK)
        rotors = rot[rows_here, :].astype(F32)
        for degree, rows in ROWS_OF.items():
            first = degree * degree
            sums = [None] * (2 * degree + 1)
            for row in rows:
                a = scaled[rows_here, row * CH : (row + 1) * CH].astype(F32)
                b = grad_dst[rows_here, row * CH : (row + 1) * CH].astype(F32)
                for n in range(2 * degree + 1):
                    at = row * LCOEF + first + n
                    r = jnp.broadcast_to(rotors[:, at : at + 1], (BLOCK, CH))
                    sums[n] = (r * a, r * b) if sums[n] is None else (sums[n][0] + r * a, sums[n][1] + r * b)
            for n in range(2 * degree + 1):
                cut = slice((first + n) * CH, (first + n + 1) * CH)
                back[rows_here, cut] = sums[n][0].astype(BF16)
                terms[rows_here, cut] = sums[n][1].astype(BF16)
        return carry

    lax.fori_loop(0, EDGES // BLOCK, turn, 0)
    chosen = hot(target[...], (16, EDGES), 0)
    for first in range(0, FULL, 640):
        cut = slice(first, first + 640)
        node_out[:, cut] = mm(chosen, back[:, cut])[:4].astype(BF16)
        grad_local[:, cut] = mm(chosen, terms[:, cut])[:4]


def call(kernel, name, args, outs, scratch, flops, transcendentals=0):
    moved = sum(a.size * a.dtype.itemsize for a in args)
    return pl.pallas_call(
        kernel,
        out_shape=tuple(jax.ShapeDtypeStruct(s, t) for s, t in outs),
        in_specs=[pl.BlockSpec(memory_space=pltpu.VMEM)] * len(args),
        out_specs=tuple(pl.BlockSpec(memory_space=pltpu.VMEM) for _ in outs),
        scratch_shapes=[pltpu.VMEM(s, t) for s, t in scratch],
        compiler_params=pltpu.CompilerParams(vmem_limit_bytes=VMEM_LIMIT),
        cost_estimate=pl.CostEstimate(flops=flops, bytes_accessed=moved, transcendentals=transcendentals),
        name=name,
    )(*args)


def pack_units(array, rows):
    n, _, width = array.shape
    return array.reshape(n, rows, width // CH, CH).transpose(2, 0, 1, 3).reshape(width // CH, n * rows, CH)


def local(
    node_feat, rotation, source_owner, source_row, target_row, live_count, edge_bias,
    w_m0, w_m1, w_m2, w_alpha, out_grad,
):
    me = lax.axis_index("edge")
    features = node_feat[0]
    rotor_rows = rotation[0]
    targets = target_row[0]
    live = (jnp.arange(EDGES, dtype=jnp.int32) < live_count[0, 0]).astype(jnp.int32)
    place = block_place(source_owner[0, :, 0], me) * 4 + source_row[0]

    far = jnp.concatenate([features] + [pull(features, dz=4 * a) for a in (1, 2, 3)], axis=0)
    near = jnp.concatenate([far] + [pull(far, dz=NEAR[n]) for n in (1, 2, 3)], axis=0)
    feature_pieces = x_and_core(near, 32)

    w1 = jnp.concatenate([w_m1[0], w_m1[1]], axis=1)
    w2 = jnp.concatenate([w_m2[0], w_m2[1]], axis=1)

    def packed(parts):
        return jnp.concatenate([a.reshape(-1, CH) for a in parts], axis=0)

    block = packed([pack_units(w_m0[None], 10), pack_units(w1[None], 8), pack_units(w2[None], 6)])

    def merged(blocks, rows):
        cuts, at = [], 0
        for units, depth in ((5, rows[0]), (8, rows[1]), (6, rows[2])):
            parts = [b[at : at + units * depth].reshape(units, depth, CH) for b in blocks]
            cuts.append(jnp.concatenate(parts, axis=1))
            at += units * depth
        return packed(cuts)

    far_w = merged([block] + [pull(block, dz=4 * a) for a in (1, 2, 3)], (10, 8, 6))
    near_w = merged([far_w] + [pull(far_w, dz=NEAR[n]) for n in (1, 2, 3)], (40, 32, 24))
    weight_pieces = x_and_core(near_w, W_SPLIT)

    def inverse_of(depth, rows):
        p = jnp.arange(depth, dtype=jnp.int32)
        return (block_owner(p // rows, me) * rows + p % rows)[None]

    def position_of(depth, rows):
        k = jnp.arange(depth, dtype=jnp.int32)
        return (block_place(k // rows, me) * rows + k % rows)[None]

    sizes = ((1280, 10), (1024, 8), (768, 6))
    inverses = [inverse_of(*s) for s in sizes]
    positions = [position_of(*s) for s in sizes]

    cotangent = out_grad[0]
    high = lax.reduce_precision(cotangent, 8, 7)
    own_rows = jnp.concatenate(
        [features, high.astype(BF16), (cotangent - high).astype(BF16), jnp.zeros((4, FULL), BF16)], axis=0
    )

    m0, m1, m2, turned_grad = call(
        rotate_kernel, "rotate",
        (*feature_pieces, rotor_rows, place[:, None], targets[:, None], own_rows, *inverses),
        [((160, 1280), BF16), ((320, 1024), BF16), ((320, 768), BF16), ((160, MCOEF * CH), F32)],
        [((512, FULL), BF16), ((160, FULL), BF16), ((160, FULL), BF16), ((160, FULL), F32),
         ((160, 1280), BF16), ((320, 1024), BF16), ((320, 768), BF16)],
        3_000_000_000,
    )
    outs = call(
        layer_kernel, "layer",
        (*weight_pieces, m0, m1, m2, turned_grad, rotor_rows, edge_bias[0], targets[:, None], live[:, None],
         w_alpha, place[None], *positions),
        [((64, FULL), BF16)] * 8 + [((160, 640), BF16)] * 8
        + [((160, MCOEF * CH), BF16), ((160, MCOEF * CH), BF16)],
        [((1280, 640), BF16), ((1024, 1024), BF16), ((768, 768), BF16), ((160, MCOEF * CH), BF16),
         ((160, 640), BF16), ((320, 1024), BF16), ((320, 768), BF16),
         ((160, 1280), BF16), ((320, 1024), BF16), ((320, 768), BF16),
         ((160, 1280), BF16), ((320, 1024), BF16), ((320, 768), BF16), ((160, FULL), BF16)],
        5_000_000_000, 160 * 136,
    )
    term_pieces, w0_pieces, (scaled, grad_dst) = outs[:8], outs[8:16], outs[16:]
    node_out, grad_local = call(
        nodes_kernel, "nodes", (rotor_rows, scaled, grad_dst, targets[None]),
        [((4, FULL), BF16), ((4, FULL), F32)], [((160, FULL), BF16), ((160, FULL), BF16)],
        600_000_000,
    )
    grad_remote = scatter_sum(term_pieces, 32, 16, 4)
    shard = scatter_sum(w0_pieces, 80, 40, 10)
    n_rep = lax.axis_size("rep")
    grad_w0 = shard
    for r in range(1, n_rep):
        grad_w0 = grad_w0 + lax.ppermute(shard, "rep", [(i, (i + r) % n_rep) for i in range(n_rep)])
    return node_out[None], (grad_local + grad_remote)[None], grad_w0


def solution(mesh):
    placed = (
        P("rep", "edge", None), P("rep", "edge", None), P("rep", "edge", None), P("rep", "edge"),
        P("rep", "edge"), P("rep", "edge"), P("rep", "edge", None), P("edge", None),
        P(None, "edge", None), P(None, "edge", None), P(), P("rep", "edge", None),
    )
    return jax.shard_map(
        local, mesh=mesh, in_specs=placed,
        out_specs=(P("rep", "edge", None), P("rep", "edge", None), P("edge", None)),
        check_vma=False,
    )
```

```python
import jax
import jax.numpy as jnp
from jax import lax
from jax.experimental import pallas as pl
from jax.experimental.pallas import tpu as pltpu
from jax.sharding import PartitionSpec as P

LCOEF = 25
MCOEF = 19
CH = 128
HEADS = 8
EDGES = 160
BLOCK = 16
NZ, NX = 16, 4
FULL = LCOEF * CH
ROWS_OF = {0: (0,), 1: (1, 5, 9), 2: (2, 6, 10, 13, 16), 3: (3, 7, 11, 14, 17), 4: (4, 8, 12, 15, 18)}
NEAR = (0, 1, 2, -1)
FAR_ROWS = 400
DEPTHS = (48, 32, 32)
UNITS = (5, 8, 6)
WEIGHT_ROWS = 240 + 256 + 192
TERM_ROWS = 400 + 240
VMEM_LIMIT = 56 * 2**20
F32, BF16 = jnp.float32, jnp.bfloat16


def where_to(i, dz, dx, dc):
    z, x, c = i // 8, (i // 2) % 4, i % 2
    sign = 1 - 2 * c
    return ((z + sign * dz) % NZ) * 8 + ((x + dx) % NX) * 2 + (c + dc) % 2


def pull(a, dz=0, dx=0, dc=0):
    return lax.ppermute(a, "edge", [(where_to(i, dz, dx, dc), i) for i in range(128)])


def push(a, dz=0, dx=0, dc=0):
    return lax.ppermute(a, "edge", [(i, where_to(i, dz, dx, dc)) for i in range(128)])


def block_place(owner, me):
    sign = 1 - 2 * (owner % 2)
    jz = (sign * (owner // 8 - me // 8) + 1) % NZ
    xr = ((owner // 2) % 4 - (me // 2) % 4) % NX
    cr = (owner % 2 + me % 2) % 2
    near = (jz % 4 + 3) % 4
    return cr * 16 + xr * 4 + near, jz // 4


def block_owner(place, far, me):
    cr, xr, near = place // 16, (place // 4) % 4, place % 4
    sign = 1 - 2 * ((me + cr) % 2)
    offset = (near + 1) % 4 - 1
    z = (me // 8 + sign * (4 * far + offset)) % NZ
    x = ((me // 2) % 4 + xr) % NX
    return z * 8 + x * 2 + (me % 2 + cr) % 2


def x_and_core(block):
    mine = (block,) + tuple(pull(block, dx=x) for x in (1, 2, 3))
    return mine + tuple(pull(a, dc=1) for a in mine)


def scatter_sum(pieces):
    def add(a, *more):
        total = a.astype(F32)
        for m in more:
            total = total + m.astype(F32)
        return total

    a = [add(pieces[x], push(pieces[4 + x], dc=1)).astype(BF16) for x in range(4)]
    total = add(a[0], *(push(a[x], dx=x) for x in (1, 2, 3))).astype(BF16)
    parts = [total[n * TERM_ROWS : (n + 1) * TERM_ROWS] for n in range(4)]
    total = add(parts[0], *(push(parts[n], dz=NEAR[n]) for n in (1, 2, 3))).astype(BF16)
    terms, shard = total[:400].reshape(25, 16, CH), total[400:].reshape(5, 48, CH)

    def part(n):
        return jnp.concatenate(
            [terms[:, 4 * n : 4 * n + 4].reshape(100, CH), shard[:, 10 * n : 10 * n + 10].reshape(50, CH)], axis=0
        )

    total = add(part(0), *(push(part(n), dz=4 * n) for n in (1, 2, 3)))
    return total[:100].reshape(25, 4, CH), total[100:].reshape(5, 10, CH)


def hot(index, shape, axis):
    return jnp.where(index == lax.broadcasted_iota(jnp.int32, shape, axis), F32(1), F32(0)).astype(BF16)


def mm(a, b):
    return jnp.dot(a, b, preferred_element_type=F32)


def mm_nt(a, b):
    return lax.dot_general(a, b, (((1,), (1,)), ((), ())), preferred_element_type=F32)


def frame_slot(row):
    if row < 5:
        return 0, 0, row
    if row < 13:
        return 1, ((row - 5) // 4) * EDGES, (row - 5) % 4
    return 2, ((row - 13) // 3) * EDGES, (row - 13) % 3


def rotate_kernel(*refs):
    pieces = refs[:8]
    rot, place, target, local, inv0, inv1, inv2 = refs[8:15]
    m0, m1, m2, turned_grad = refs[15:19]
    feats, srcf, dstf, gradf, n0, n1, n2 = refs[19:]
    for k, piece in enumerate(pieces):
        for near in range(4):
            row = k * 64 + near * 16
            for u in range(LCOEF):
                at = near * FAR_ROWS + u * 16
                feats[row : row + 16, u * CH : (u + 1) * CH] = piece[at : at + 16, :]
    source_hot = hot(place[...], (EDGES, 512), 1)
    t = target[...]
    lanes = lax.broadcasted_iota(jnp.int32, (EDGES, 16), 1)
    feat_hot = jnp.where(lanes == t, F32(1), F32(0)).astype(BF16)
    grad_hot = jnp.where((lanes == t + 4) | (lanes == t + 8), F32(1), F32(0)).astype(BF16)
    for first in range(0, FULL, 640):
        cut = slice(first, first + 640)
        srcf[:, cut] = mm(source_hot, feats[:, cut]).astype(BF16)
        dstf[:, cut] = mm(feat_hot, local[:, cut]).astype(BF16)
        gradf[:, cut] = mm(grad_hot, local[:, cut])

    stacked = (n0, n1, n2)

    def turn(step, carry):
        e0 = pl.multiple_of(step * BLOCK, BLOCK)
        rows_here = pl.ds(e0, BLOCK)
        rotors = rot[rows_here, :].astype(F32)
        for degree, rows in ROWS_OF.items():
            sums = [None] * len(rows)
            for col in range(degree * degree, (degree + 1) ** 2):
                cut = slice(col * CH, (col + 1) * CH)
                s, d, g = srcf[rows_here, cut].astype(F32), dstf[rows_here, cut].astype(F32), gradf[rows_here, cut]
                for n, row in enumerate(rows):
                    r = jnp.broadcast_to(rotors[:, row * LCOEF + col : row * LCOEF + col + 1], (BLOCK, CH))
                    terms = (r * s, r * d, r * g)
                    sums[n] = terms if sums[n] is None else tuple(a + b for a, b in zip(sums[n], terms))
            for n, row in enumerate(rows):
                array, base, column = frame_slot(row)
                out = stacked[array]
                out_rows = pl.ds(pl.multiple_of(base + e0, BLOCK), BLOCK)
                out[out_rows, column * 256 : column * 256 + CH] = sums[n][0].astype(BF16)
                out[out_rows, column * 256 + CH : column * 256 + 256] = sums[n][1].astype(BF16)
                turned_grad[rows_here, row * CH : (row + 1) * CH] = sums[n][2]
        return carry

    lax.fori_loop(0, EDGES // BLOCK, turn, 0)
    for natural, ordered, inverse in ((n0, m0, inv0), (n1, m1, inv1), (n2, m2, inv2)):
        depth = natural.shape[1]
        for first in range(0, ordered.shape[1], 256):
            cut = slice(first, first + 256)
            ordered[:, cut] = mm(natural[...], hot(inverse[:, cut], (depth, 256), 0)).astype(BF16)


def layer_kernel(*refs):
    pieces = refs[:8]
    m0, m1, m2, turned_grad, rot, bias, target, live_ref, alpha_ref, place, pos0, pos1, pos2 = refs[8:21]
    terms_out = refs[21:29]
    scaled_out, grad_dst = refs[29:31]
    w0, w1, w2, values, d0, d1, d2, p0, p1, p2, g0, g1, g2, src_terms = refs[31:]
    for k, piece in enumerate(pieces):
        for near in range(4):
            at = near * WEIGHT_ROWS
            for out, units, rows in zip((w0, w1, w2), UNITS, DEPTHS):
                to = (k * 4 + near) * rows
                for u in range(units):
                    out[to : to + rows, u * CH : (u + 1) * CH] = piece[at : at + rows, :]
                    at += rows
    z0 = mm(m0[...], w0[...])
    for row in range(5):
        values[:, row * CH : (row + 1) * CH] = z0[:, row * CH : (row + 1) * CH].astype(BF16)
    z1 = mm(m1[...], w1[...])
    values[:, 5 * CH : 9 * CH] = (z1[:EDGES, :512] - z1[EDGES:, 512:]).astype(BF16)
    values[:, 9 * CH : 13 * CH] = (z1[EDGES:, :512] + z1[:EDGES, 512:]).astype(BF16)
    z2 = mm(m2[...], w2[...])
    values[:, 13 * CH : 16 * CH] = (z2[:EDGES, :384] - z2[EDGES:, 384:]).astype(BF16)
    values[:, 16 * CH : 19 * CH] = (z2[EDGES:, :384] + z2[:EDGES, 384:]).astype(BF16)

    v = z0[:, :CH]
    sigma = 1.0 / (1.0 + jnp.exp(-v))
    alpha = alpha_ref[...]
    logits = bias[...] + mm((v * sigma).astype(BF16), alpha)
    live = live_ref[...] > 0
    t = target[...]
    members = [live & (t == n) for n in range(4)]

    def over_targets(array, empty, reduce):
        result = jnp.zeros((EDGES, HEADS), F32)
        for member in members:
            one = reduce(jnp.where(member, array, F32(empty)), axis=0, keepdims=True)
            result = jnp.where(member, one, result)
        return result

    top = over_targets(logits, -1e30, jnp.max)
    expo = jnp.where(live, jnp.exp(jnp.where(live, logits - top, F32(0))), F32(0))
    denom = jnp.where(live, over_targets(expo, 0.0, jnp.sum), F32(1))
    attn = expo / denom
    head_of = (
        lax.broadcasted_iota(jnp.int32, (HEADS, CH), 1) // (CH // HEADS)
        == lax.broadcasted_iota(jnp.int32, (HEADS, CH), 0)
    )
    spread = jnp.where(head_of, F32(1), F32(0))
    scale = jnp.dot(attn, spread, precision=lax.Precision.HIGHEST, preferred_element_type=F32)
    dscale = jnp.zeros((EDGES, CH), F32)
    for row in range(MCOEF):
        cut = slice(row * CH, (row + 1) * CH)
        value = values[:, cut].astype(F32)
        dscale = dscale + turned_grad[:, cut] * value
        scaled_out[:, cut] = (scale * value).astype(BF16)
    dattn = lax.dot_general(
        dscale, spread, (((1,), (1,)), ((), ())), precision=lax.Precision.HIGHEST, preferred_element_type=F32
    )
    dlogits = attn * (dattn - over_targets(attn * dattn, 0.0, jnp.sum))
    dscalars = lax.dot_general(
        dlogits, alpha.astype(F32), (((1,), (1,)), ((), ())), precision=lax.Precision.HIGHEST,
        preferred_element_type=F32,
    ).astype(BF16).astype(F32)
    dv = dscalars * (sigma * (1.0 + v * (1.0 - sigma)))
    for row in range(MCOEF):
        cut = slice(row * CH, (row + 1) * CH)
        dvalue = (scale * turned_grad[:, cut]).astype(BF16)
        if row == 0:
            dvalue = (dvalue.astype(F32) + dv).astype(BF16)
        if row < 5:
            d0[:, cut] = dvalue
            continue
        out, width, column, plus = (d1, 512, (row - 5) % 4, row < 9) if row < 13 else (d2, 384, (row - 13) % 3, row < 16)
        a, b = column * CH, width + column * CH
        if plus:
            out[:EDGES, a : a + CH] = dvalue
            out[EDGES:, b : b + CH] = -dvalue
        else:
            out[EDGES:, a : a + CH] = dvalue
            out[:EDGES, b : b + CH] = dvalue
    dw = lax.dot_general(m0[...], d0[...], (((0,), (0,)), ((), ())), preferred_element_type=F32)
    for k in range(8):
        for near in range(4):
            row = (k * 4 + near) * 48
            for u in range(5):
                at = near * TERM_ROWS + 400 + u * 48
                terms_out[k][at : at + 48, :] = dw[row : row + 48, u * CH : (u + 1) * CH].astype(BF16)
    for d, w, p, g, pos in ((d0, w0, p0, g0, pos0), (d1, w1, p1, g1, pos1), (d2, w2, p2, g2, pos2)):
        p[...] = mm_nt(d[...], w[...]).astype(BF16)
        for first in range(0, g.shape[1], 256):
            cut = slice(first, first + 256)
            g[:, cut] = mm(p[...], hot(pos[:, cut], (w.shape[0], 256), 0)).astype(BF16)
    stacked = (g0, g1, g2)
    for row in range(MCOEF):
        array, base, column = frame_slot(row)
        grad_dst[:, row * CH : (row + 1) * CH] = stacked[array][base : base + EDGES, column * 256 + CH : column * 256 + 256]

    def turn(step, carry):
        e0 = pl.multiple_of(step * BLOCK, BLOCK)
        rows_here = pl.ds(e0, BLOCK)
        rotors = rot[rows_here, :].astype(F32)
        for degree, rows in ROWS_OF.items():
            first = degree * degree
            sums = [None] * (2 * degree + 1)
            for row in rows:
                array, base, column = frame_slot(row)
                s = stacked[array][pl.ds(pl.multiple_of(base + e0, BLOCK), BLOCK), column * 256 : column * 256 + CH]
                s = s.astype(F32)
                for n in range(2 * degree + 1):
                    at = row * LCOEF + first + n
                    term = jnp.broadcast_to(rotors[:, at : at + 1], (BLOCK, CH)) * s
                    sums[n] = term if sums[n] is None else sums[n] + term
            for n in range(2 * degree + 1):
                src_terms[rows_here, (first + n) * CH : (first + n + 1) * CH] = sums[n].astype(BF16)
        return carry

    lax.fori_loop(0, EDGES // BLOCK, turn, 0)
    for k in range(8):
        chosen = hot(place[...] - k * 64, (64, EDGES), 0)
        for first in range(0, FULL, 640):
            block = mm(chosen, src_terms[:, first : first + 640]).astype(BF16)
            for near in range(4):
                for n in range(5):
                    at = near * TERM_ROWS + (first // CH + n) * 16
                    terms_out[k][at : at + 16, :] = block[near * 16 : near * 16 + 16, n * CH : (n + 1) * CH]


def nodes_kernel(rot, scaled, grad_dst, target, node_out, grad_local, back, terms):
    def turn(step, carry):
        e0 = pl.multiple_of(step * BLOCK, BLOCK)
        rows_here = pl.ds(e0, BLOCK)
        rotors = rot[rows_here, :].astype(F32)
        for degree, rows in ROWS_OF.items():
            first = degree * degree
            sums = [None] * (2 * degree + 1)
            for row in rows:
                a = scaled[rows_here, row * CH : (row + 1) * CH].astype(F32)
                b = grad_dst[rows_here, row * CH : (row + 1) * CH].astype(F32)
                for n in range(2 * degree + 1):
                    at = row * LCOEF + first + n
                    r = jnp.broadcast_to(rotors[:, at : at + 1], (BLOCK, CH))
                    sums[n] = (r * a, r * b) if sums[n] is None else (sums[n][0] + r * a, sums[n][1] + r * b)
            for n in range(2 * degree + 1):
                cut = slice((first + n) * CH, (first + n + 1) * CH)
                back[rows_here, cut] = sums[n][0].astype(BF16)
                terms[rows_here, cut] = sums[n][1].astype(BF16)
        return carry

    lax.fori_loop(0, EDGES // BLOCK, turn, 0)
    chosen = hot(target[...], (16, EDGES), 0)
    for first in range(0, FULL, 640):
        cut = slice(first, first + 640)
        node_out[:, cut] = mm(chosen, back[:, cut])[:4].astype(BF16)
        grad_local[:, cut] = mm(chosen, terms[:, cut])[:4]


def call(kernel, name, args, outs, scratch, flops, transcendentals=0):
    moved = sum(a.size * a.dtype.itemsize for a in args)
    return pl.pallas_call(
        kernel,
        out_shape=tuple(jax.ShapeDtypeStruct(s, t) for s, t in outs),
        in_specs=[pl.BlockSpec(memory_space=pltpu.VMEM)] * len(args),
        out_specs=tuple(pl.BlockSpec(memory_space=pltpu.VMEM) for _ in outs),
        scratch_shapes=[pltpu.VMEM(s, t) for s, t in scratch],
        compiler_params=pltpu.CompilerParams(vmem_limit_bytes=VMEM_LIMIT),
        cost_estimate=pl.CostEstimate(flops=flops, bytes_accessed=moved, transcendentals=transcendentals),
        name=name,
    )(*args)


def units_of(array):
    rows, width = array.shape
    return array.reshape(rows, width // CH, CH).transpose(1, 0, 2).reshape(-1, CH)


def local(
    node_feat, rotation, source_owner, source_row, target_row, live_count, edge_bias,
    w_m0, w_m1, w_m2, w_alpha, out_grad,
):
    me = lax.axis_index("edge")
    features = node_feat[0]
    rotor_rows = rotation[0]
    targets = target_row[0]
    live = (jnp.arange(EDGES, dtype=jnp.int32) < live_count[0, 0]).astype(jnp.int32)
    block, far = block_place(source_owner[0, :, 0], me)
    place = block * 16 + far * 4 + source_row[0]

    w1 = jnp.concatenate([w_m1[0], w_m1[1]], axis=1)
    w2 = jnp.concatenate([w_m2[0], w_m2[1]], axis=1)
    shards = (features, w_m0, w1, w2)
    own = jnp.concatenate([units_of(a) for a in shards], axis=0)
    blocks = [own] + [pull(own, dz=4 * a) for a in (1, 2, 3)]
    merged, at = [], 0
    for shard, depth in zip(shards, (16,) + DEPTHS):
        rows, units = shard.shape[0], shard.shape[1] // CH
        parts = [b[at : at + units * rows].reshape(units, rows, CH) for b in blocks]
        if depth > 4 * rows:
            parts.append(jnp.zeros((units, depth - 4 * rows, CH), BF16))
        merged.append(jnp.concatenate(parts, axis=1).reshape(units * depth, CH))
        at += units * rows
    far_block = jnp.concatenate(merged, axis=0)
    blocks = [far_block] + [pull(far_block, dz=NEAR[n]) for n in (1, 2, 3)]
    feature_pieces = x_and_core(jnp.concatenate([b[:FAR_ROWS] for b in blocks], axis=0))
    weight_pieces = x_and_core(jnp.concatenate([b[FAR_ROWS:] for b in blocks], axis=0))

    def inverse_of(rows, depth):
        p = jnp.arange(32 * depth, dtype=jnp.int32)
        inside = p % depth
        owner = block_owner(p // depth, inside // rows, me)
        return jnp.where(inside < 4 * rows, owner * rows + inside % rows, -1)[None]

    def position_of(rows, depth):
        k = jnp.arange(128 * rows, dtype=jnp.int32)
        block, far = block_place(k // rows, me)
        return (block * depth + far * rows + k % rows)[None]

    sizes = tuple(zip((10, 8, 6), DEPTHS))
    inverses = [inverse_of(*s) for s in sizes]
    positions = [position_of(*s) for s in sizes]

    cotangent = out_grad[0]
    high = lax.reduce_precision(cotangent, 8, 7)
    own_rows = jnp.concatenate(
        [features, high.astype(BF16), (cotangent - high).astype(BF16), jnp.zeros((4, FULL), BF16)], axis=0
    )

    m0, m1, m2, turned_grad = call(
        rotate_kernel, "rotate",
        (*feature_pieces, rotor_rows, place[:, None], targets[:, None], own_rows, *inverses),
        [((160, 1536), BF16), ((320, 1024), BF16), ((320, 1024), BF16), ((160, MCOEF * CH), F32)],
        [((512, FULL), BF16), ((160, FULL), BF16), ((160, FULL), BF16), ((160, FULL), F32),
         ((160, 1280), BF16), ((320, 1024), BF16), ((320, 768), BF16)],
        3_000_000_000,
    )
    outs = call(
        layer_kernel, "layer",
        (*weight_pieces, m0, m1, m2, turned_grad, rotor_rows, edge_bias[0], targets[:, None], live[:, None],
         w_alpha, place[None], *positions),
        [((4 * TERM_ROWS, CH), BF16)] * 8 + [((160, MCOEF * CH), BF16), ((160, MCOEF * CH), BF16)],
        [((1536, 640), BF16), ((1024, 1024), BF16), ((1024, 768), BF16), ((160, MCOEF * CH), BF16),
         ((160, 640), BF16), ((320, 1024), BF16), ((320, 768), BF16),
         ((160, 1536), BF16), ((320, 1024), BF16), ((320, 1024), BF16),
         ((160, 1280), BF16), ((320, 1024), BF16), ((320, 768), BF16), ((160, FULL), BF16)],
        5_000_000_000, 160 * 136,
    )
    term_pieces, (scaled, grad_dst) = outs[:8], outs[8:]
    node_out, grad_local = call(
        nodes_kernel, "nodes", (rotor_rows, scaled, grad_dst, targets[None]),
        [((4, FULL), BF16), ((4, FULL), F32)], [((160, FULL), BF16), ((160, FULL), BF16)],
        600_000_000,
    )
    terms, shard = scatter_sum(term_pieces)
    grad_remote = terms.transpose(1, 0, 2).reshape(4, FULL)
    shard = shard.transpose(1, 0, 2).reshape(10, 640)
    n_rep = lax.axis_size("rep")
    grad_w0 = shard
    for r in range(1, n_rep):
        grad_w0 = grad_w0 + lax.ppermute(shard, "rep", [(i, (i + r) % n_rep) for i in range(n_rep)])
    return node_out[None], (grad_local + grad_remote)[None], grad_w0


def solution(mesh):
    placed = (
        P("rep", "edge", None), P("rep", "edge", None), P("rep", "edge", None), P("rep", "edge"),
        P("rep", "edge"), P("rep", "edge"), P("rep", "edge", None), P("edge", None),
        P(None, "edge", None), P(None, "edge", None), P(), P("rep", "edge", None),
    )
    return jax.shard_map(
        local, mesh=mesh, in_specs=placed,
        out_specs=(P("rep", "edge", None), P("rep", "edge", None), P("edge", None)),
        check_vma=False,
    )
```

```python
import jax
import jax.numpy as jnp
from jax import lax
from jax.experimental import pallas as pl
from jax.experimental.pallas import tpu as pltpu
from jax.sharding import PartitionSpec as P

LCOEF = 25
MCOEF = 19
CH = 128
HEADS = 8
EDGES = 160
BLOCK = 16
NZ, NX = 16, 4
FULL = LCOEF * CH
ROWS_OF = {0: (0,), 1: (1, 5, 9), 2: (2, 6, 10, 13, 16), 3: (3, 7, 11, 14, 17), 4: (4, 8, 12, 15, 18)}
NEAR = (0, 1, 2, -1)
FAR_ROWS = 400
DEPTHS = (48, 32, 32)
UNITS = (5, 8, 6)
WEIGHT_ROWS = 240 + 256 + 192
TERM_ROWS = 400 + 240
VMEM_LIMIT = 56 * 2**20
F32, BF16 = jnp.float32, jnp.bfloat16


def where_to(i, dz, dx, dc):
    z, x, c = i // 8, (i // 2) % 4, i % 2
    sign = 1 - 2 * c
    return ((z + sign * dz) % NZ) * 8 + ((x + dx) % NX) * 2 + (c + dc) % 2


def pull(a, dz=0, dx=0, dc=0):
    return lax.ppermute(a, "edge", [(where_to(i, dz, dx, dc), i) for i in range(128)])


def push(a, dz=0, dx=0, dc=0):
    return lax.ppermute(a, "edge", [(i, where_to(i, dz, dx, dc)) for i in range(128)])


def block_place(owner, me):
    sign = 1 - 2 * (owner % 2)
    jz = (sign * (owner // 8 - me // 8) + 1) % NZ
    xr = ((owner // 2) % 4 - (me // 2) % 4) % NX
    cr = (owner % 2 + me % 2) % 2
    near = (jz % 4 + 3) % 4
    return cr * 16 + xr * 4 + near, jz // 4


def block_owner(place, far, me):
    cr, xr, near = place // 16, (place // 4) % 4, place % 4
    sign = 1 - 2 * ((me + cr) % 2)
    offset = (near + 1) % 4 - 1
    z = (me // 8 + sign * (4 * far + offset)) % NZ
    x = ((me // 2) % 4 + xr) % NX
    return z * 8 + x * 2 + (me % 2 + cr) % 2


def x_pieces(block):
    return (block,) + tuple(pull(block, dx=x) for x in (1, 2, 3))


def scatter_sum(pieces, beside):
    def add(a, *more):
        total = a.astype(F32)
        for m in more:
            total = total + m.astype(F32)
        return total

    a = [add(pieces[x], push(pieces[4 + x], dc=1)).astype(BF16) for x in range(4)]
    arrived, beside = lax.optimization_barrier(([push(a[x], dx=x) for x in (1, 2, 3)], beside))
    total = add(a[0], *arrived).astype(BF16)
    parts = [total[n * TERM_ROWS : (n + 1) * TERM_ROWS] for n in range(4)]
    total = add(parts[0], *(push(parts[n], dz=NEAR[n]) for n in (1, 2, 3))).astype(BF16)
    terms, shard = total[:400].reshape(25, 16, CH), total[400:].reshape(5, 48, CH)

    def part(n):
        return jnp.concatenate(
            [terms[:, 4 * n : 4 * n + 4].reshape(100, CH), shard[:, 10 * n : 10 * n + 10].reshape(50, CH)], axis=0
        )

    total = add(part(0), *(push(part(n), dz=4 * n) for n in (1, 2, 3)))
    return total[:100].reshape(25, 4, CH), total[100:].reshape(5, 10, CH), beside


def hot(index, shape, axis):
    return jnp.where(index == lax.broadcasted_iota(jnp.int32, shape, axis), F32(1), F32(0)).astype(BF16)


def mm(a, b):
    return jnp.dot(a, b, preferred_element_type=F32)


def mm_nt(a, b):
    return lax.dot_general(a, b, (((1,), (1,)), ((), ())), preferred_element_type=F32)


def frame_slot(row):
    if row < 5:
        return 0, 0, row
    if row < 13:
        return 1, ((row - 5) // 4) * EDGES, (row - 5) % 4
    return 2, ((row - 13) // 3) * EDGES, (row - 13) % 3


def rotate_kernel(*refs):
    pieces = refs[:8]
    rot, place, target, local, inv0, inv1, inv2 = refs[8:15]
    m0, m1, m2, turned_grad = refs[15:19]
    feats, srcf, dstf, gradf, n0, n1, n2 = refs[19:]
    for k, piece in enumerate(pieces):
        for near in range(4):
            row = k * 64 + near * 16
            for u in range(LCOEF):
                at = near * FAR_ROWS + u * 16
                feats[row : row + 16, u * CH : (u + 1) * CH] = piece[at : at + 16, :]
    source_hot = hot(place[...], (EDGES, 512), 1)
    t = target[...]
    lanes = lax.broadcasted_iota(jnp.int32, (EDGES, 16), 1)
    feat_hot = jnp.where(lanes == t, F32(1), F32(0)).astype(BF16)
    grad_hot = jnp.where((lanes == t + 4) | (lanes == t + 8), F32(1), F32(0)).astype(BF16)
    for first in range(0, FULL, 640):
        cut = slice(first, first + 640)
        srcf[:, cut] = mm(source_hot, feats[:, cut]).astype(BF16)
        dstf[:, cut] = mm(feat_hot, local[:, cut]).astype(BF16)
        gradf[:, cut] = mm(grad_hot, local[:, cut])

    stacked = (n0, n1, n2)

    def turn(step, carry):
        e0 = pl.multiple_of(step * BLOCK, BLOCK)
        rows_here = pl.ds(e0, BLOCK)
        rotors = rot[rows_here, :].astype(F32)
        for degree, rows in ROWS_OF.items():
            sums = [None] * len(rows)
            for col in range(degree * degree, (degree + 1) ** 2):
                cut = slice(col * CH, (col + 1) * CH)
                s, d, g = srcf[rows_here, cut].astype(F32), dstf[rows_here, cut].astype(F32), gradf[rows_here, cut]
                for n, row in enumerate(rows):
                    r = jnp.broadcast_to(rotors[:, row * LCOEF + col : row * LCOEF + col + 1], (BLOCK, CH))
                    terms = (r * s, r * d, r * g)
                    sums[n] = terms if sums[n] is None else tuple(a + b for a, b in zip(sums[n], terms))
            for n, row in enumerate(rows):
                array, base, column = frame_slot(row)
                out = stacked[array]
                out_rows = pl.ds(pl.multiple_of(base + e0, BLOCK), BLOCK)
                out[out_rows, column * 256 : column * 256 + CH] = sums[n][0].astype(BF16)
                out[out_rows, column * 256 + CH : column * 256 + 256] = sums[n][1].astype(BF16)
                turned_grad[rows_here, row * CH : (row + 1) * CH] = sums[n][2]
        return carry

    lax.fori_loop(0, EDGES // BLOCK, turn, 0)
    for natural, ordered, inverse in ((n0, m0, inv0), (n1, m1, inv1), (n2, m2, inv2)):
        depth = natural.shape[1]
        for first in range(0, ordered.shape[1], 256):
            cut = slice(first, first + 256)
            ordered[:, cut] = mm(natural[...], hot(inverse[:, cut], (depth, 256), 0)).astype(BF16)


def layer_kernel(*refs):
    pieces = refs[:8]
    m0, m1, m2, turned_grad, rot, bias, target, live_ref, alpha_ref, place, pos0, pos1, pos2 = refs[8:21]
    terms_out = refs[21:29]
    scaled_out, grad_dst = refs[29:31]
    w0, w1, w2, values, d0, d1, d2, p0, p1, p2, g0, g1, g2, src_terms = refs[31:]
    for k, piece in enumerate(pieces):
        for near in range(4):
            at = near * WEIGHT_ROWS
            for out, units, rows in zip((w0, w1, w2), UNITS, DEPTHS):
                to = (k * 4 + near) * rows
                for u in range(units):
                    out[to : to + rows, u * CH : (u + 1) * CH] = piece[at : at + rows, :]
                    at += rows
    z0 = mm(m0[...], w0[...])
    for row in range(5):
        values[:, row * CH : (row + 1) * CH] = z0[:, row * CH : (row + 1) * CH].astype(BF16)
    z1 = mm(m1[...], w1[...])
    values[:, 5 * CH : 9 * CH] = (z1[:EDGES, :512] - z1[EDGES:, 512:]).astype(BF16)
    values[:, 9 * CH : 13 * CH] = (z1[EDGES:, :512] + z1[:EDGES, 512:]).astype(BF16)
    z2 = mm(m2[...], w2[...])
    values[:, 13 * CH : 16 * CH] = (z2[:EDGES, :384] - z2[EDGES:, 384:]).astype(BF16)
    values[:, 16 * CH : 19 * CH] = (z2[EDGES:, :384] + z2[:EDGES, 384:]).astype(BF16)

    v = z0[:, :CH]
    sigma = 1.0 / (1.0 + jnp.exp(-v))
    alpha = alpha_ref[...]
    logits = bias[...] + mm((v * sigma).astype(BF16), alpha)
    live = live_ref[...] > 0
    t = target[...]
    members = [live & (t == n) for n in range(4)]

    def over_targets(array, empty, reduce):
        result = jnp.zeros((EDGES, HEADS), F32)
        for member in members:
            one = reduce(jnp.where(member, array, F32(empty)), axis=0, keepdims=True)
            result = jnp.where(member, one, result)
        return result

    top = over_targets(logits, -1e30, jnp.max)
    expo = jnp.where(live, jnp.exp(jnp.where(live, logits - top, F32(0))), F32(0))
    denom = jnp.where(live, over_targets(expo, 0.0, jnp.sum), F32(1))
    attn = expo / denom
    head_of = (
        lax.broadcasted_iota(jnp.int32, (HEADS, CH), 1) // (CH // HEADS)
        == lax.broadcasted_iota(jnp.int32, (HEADS, CH), 0)
    )
    spread = jnp.where(head_of, F32(1), F32(0))
    scale = jnp.dot(attn, spread, precision=lax.Precision.HIGHEST, preferred_element_type=F32)
    dscale = jnp.zeros((EDGES, CH), F32)
    for row in range(MCOEF):
        cut = slice(row * CH, (row + 1) * CH)
        value = values[:, cut].astype(F32)
        dscale = dscale + turned_grad[:, cut] * value
        scaled_out[:, cut] = (scale * value).astype(BF16)
    dattn = lax.dot_general(
        dscale, spread, (((1,), (1,)), ((), ())), precision=lax.Precision.HIGHEST, preferred_element_type=F32
    )
    dlogits = attn * (dattn - over_targets(attn * dattn, 0.0, jnp.sum))
    dscalars = lax.dot_general(
        dlogits, alpha.astype(F32), (((1,), (1,)), ((), ())), precision=lax.Precision.HIGHEST,
        preferred_element_type=F32,
    ).astype(BF16).astype(F32)
    dv = dscalars * (sigma * (1.0 + v * (1.0 - sigma)))
    for row in range(MCOEF):
        cut = slice(row * CH, (row + 1) * CH)
        dvalue = (scale * turned_grad[:, cut]).astype(BF16)
        if row == 0:
            dvalue = (dvalue.astype(F32) + dv).astype(BF16)
        if row < 5:
            d0[:, cut] = dvalue
            continue
        out, width, column, plus = (d1, 512, (row - 5) % 4, row < 9) if row < 13 else (d2, 384, (row - 13) % 3, row < 16)
        a, b = column * CH, width + column * CH
        if plus:
            out[:EDGES, a : a + CH] = dvalue
            out[EDGES:, b : b + CH] = -dvalue
        else:
            out[EDGES:, a : a + CH] = dvalue
            out[:EDGES, b : b + CH] = dvalue
    dw = lax.dot_general(m0[...], d0[...], (((0,), (0,)), ((), ())), preferred_element_type=F32)
    for k in range(8):
        for near in range(4):
            row = (k * 4 + near) * 48
            for u in range(5):
                at = near * TERM_ROWS + 400 + u * 48
                terms_out[k][at : at + 48, :] = dw[row : row + 48, u * CH : (u + 1) * CH].astype(BF16)
    for d, w, p, g, pos in ((d0, w0, p0, g0, pos0), (d1, w1, p1, g1, pos1), (d2, w2, p2, g2, pos2)):
        p[...] = mm_nt(d[...], w[...]).astype(BF16)
        for first in range(0, g.shape[1], 256):
            cut = slice(first, first + 256)
            g[:, cut] = mm(p[...], hot(pos[:, cut], (w.shape[0], 256), 0)).astype(BF16)
    stacked = (g0, g1, g2)
    for row in range(MCOEF):
        array, base, column = frame_slot(row)
        grad_dst[:, row * CH : (row + 1) * CH] = stacked[array][base : base + EDGES, column * 256 + CH : column * 256 + 256]

    def turn(step, carry):
        e0 = pl.multiple_of(step * BLOCK, BLOCK)
        rows_here = pl.ds(e0, BLOCK)
        rotors = rot[rows_here, :].astype(F32)
        for degree, rows in ROWS_OF.items():
            first = degree * degree
            sums = [None] * (2 * degree + 1)
            for row in rows:
                array, base, column = frame_slot(row)
                s = stacked[array][pl.ds(pl.multiple_of(base + e0, BLOCK), BLOCK), column * 256 : column * 256 + CH]
                s = s.astype(F32)
                for n in range(2 * degree + 1):
                    at = row * LCOEF + first + n
                    term = jnp.broadcast_to(rotors[:, at : at + 1], (BLOCK, CH)) * s
                    sums[n] = term if sums[n] is None else sums[n] + term
            for n in range(2 * degree + 1):
                src_terms[rows_here, (first + n) * CH : (first + n + 1) * CH] = sums[n].astype(BF16)
        return carry

    lax.fori_loop(0, EDGES // BLOCK, turn, 0)
    chosen = hot(place[...], (512, EDGES), 0)
    for first in range(0, FULL, 640):
        block = mm(chosen, src_terms[:, first : first + 640]).astype(BF16)
        for k in range(8):
            for near in range(4):
                row = k * 64 + near * 16
                for n in range(5):
                    at = near * TERM_ROWS + (first // CH + n) * 16
                    terms_out[k][at : at + 16, :] = block[row : row + 16, n * CH : (n + 1) * CH]


def nodes_kernel(rot, scaled, grad_dst, target, node_out, grad_local, back, terms):
    def turn(step, carry):
        e0 = pl.multiple_of(step * BLOCK, BLOCK)
        rows_here = pl.ds(e0, BLOCK)
        rotors = rot[rows_here, :].astype(F32)
        for degree, rows in ROWS_OF.items():
            first = degree * degree
            sums = [None] * (2 * degree + 1)
            for row in rows:
                a = scaled[rows_here, row * CH : (row + 1) * CH].astype(F32)
                b = grad_dst[rows_here, row * CH : (row + 1) * CH].astype(F32)
                for n in range(2 * degree + 1):
                    at = row * LCOEF + first + n
                    r = jnp.broadcast_to(rotors[:, at : at + 1], (BLOCK, CH))
                    sums[n] = (r * a, r * b) if sums[n] is None else (sums[n][0] + r * a, sums[n][1] + r * b)
            for n in range(2 * degree + 1):
                cut = slice((first + n) * CH, (first + n + 1) * CH)
                back[rows_here, cut] = sums[n][0].astype(BF16)
                terms[rows_here, cut] = sums[n][1].astype(BF16)
        return carry

    lax.fori_loop(0, EDGES // BLOCK, turn, 0)
    chosen = hot(target[...], (16, EDGES), 0)
    for first in range(0, FULL, 640):
        cut = slice(first, first + 640)
        node_out[:, cut] = mm(chosen, back[:, cut])[:4].astype(BF16)
        grad_local[:, cut] = mm(chosen, terms[:, cut])[:4]


def call(kernel, name, args, outs, scratch, flops, transcendentals=0):
    moved = sum(a.size * a.dtype.itemsize for a in args)
    return pl.pallas_call(
        kernel,
        out_shape=tuple(jax.ShapeDtypeStruct(s, t) for s, t in outs),
        in_specs=[pl.BlockSpec(memory_space=pltpu.VMEM)] * len(args),
        out_specs=tuple(pl.BlockSpec(memory_space=pltpu.VMEM) for _ in outs),
        scratch_shapes=[pltpu.VMEM(s, t) for s, t in scratch],
        compiler_params=pltpu.CompilerParams(vmem_limit_bytes=VMEM_LIMIT),
        cost_estimate=pl.CostEstimate(flops=flops, bytes_accessed=moved, transcendentals=transcendentals),
        name=name,
    )(*args)


def units_of(array):
    rows, width = array.shape
    return array.reshape(rows, width // CH, CH).transpose(1, 0, 2).reshape(-1, CH)


def local(
    node_feat, rotation, source_owner, source_row, target_row, live_count, edge_bias,
    w_m0, w_m1, w_m2, w_alpha, out_grad,
):
    me = lax.axis_index("edge")
    features = node_feat[0]
    rotor_rows = rotation[0]
    targets = target_row[0]
    live = (jnp.arange(EDGES, dtype=jnp.int32) < live_count[0, 0]).astype(jnp.int32)
    block, far = block_place(source_owner[0, :, 0], me)
    place = block * 16 + far * 4 + source_row[0]

    w1 = jnp.concatenate([w_m1[0], w_m1[1]], axis=1)
    w2 = jnp.concatenate([w_m2[0], w_m2[1]], axis=1)
    shards = (features, w_m0, w1, w2)
    own = jnp.concatenate([units_of(a) for a in shards], axis=0)
    blocks = [own] + [pull(own, dz=4 * a) for a in (1, 2, 3)]
    merged, at = [], 0
    for shard, depth in zip(shards, (16,) + DEPTHS):
        rows, units = shard.shape[0], shard.shape[1] // CH
        parts = [b[at : at + units * rows].reshape(units, rows, CH) for b in blocks]
        if depth > 4 * rows:
            parts.append(jnp.zeros((units, depth - 4 * rows, CH), BF16))
        merged.append(jnp.concatenate(parts, axis=1).reshape(units * depth, CH))
        at += units * rows
    far_block = jnp.concatenate(merged, axis=0)
    blocks = [far_block] + [pull(far_block, dz=NEAR[n]) for n in (1, 2, 3)]
    feature_x = x_pieces(jnp.concatenate([b[:FAR_ROWS] for b in blocks], axis=0))
    weight_x = x_pieces(jnp.concatenate([b[FAR_ROWS:] for b in blocks], axis=0))
    feature_pieces = feature_x + tuple(pull(a, dc=1) for a in feature_x)

    def inverse_of(rows, depth):
        p = jnp.arange(32 * depth, dtype=jnp.int32)
        inside = p % depth
        owner = block_owner(p // depth, inside // rows, me)
        return jnp.where(inside < 4 * rows, owner * rows + inside % rows, -1)[None]

    def position_of(rows, depth):
        k = jnp.arange(128 * rows, dtype=jnp.int32)
        block, far = block_place(k // rows, me)
        return (block * depth + far * rows + k % rows)[None]

    sizes = tuple(zip((10, 8, 6), DEPTHS))
    inverses = [inverse_of(*s) for s in sizes]
    positions = [position_of(*s) for s in sizes]

    cotangent = out_grad[0]
    high = lax.reduce_precision(cotangent, 8, 7)
    own_rows = jnp.concatenate(
        [features, high.astype(BF16), (cotangent - high).astype(BF16), jnp.zeros((4, FULL), BF16)], axis=0
    )

    m0, m1, m2, turned_grad = call(
        rotate_kernel, "rotate",
        (*feature_pieces, rotor_rows, place[:, None], targets[:, None], own_rows, *inverses),
        [((160, 1536), BF16), ((320, 1024), BF16), ((320, 1024), BF16), ((160, MCOEF * CH), F32)],
        [((512, FULL), BF16), ((160, FULL), BF16), ((160, FULL), BF16), ((160, FULL), F32),
         ((160, 1280), BF16), ((320, 1024), BF16), ((320, 768), BF16)],
        3_000_000_000,
    )
    turned, others = lax.optimization_barrier(((m0, m1, m2, turned_grad), weight_x[1:]))
    m0, m1, m2, turned_grad = turned
    weight_x = weight_x[:1] + tuple(others)
    weight_pieces = weight_x + tuple(pull(a, dc=1) for a in weight_x)
    outs = call(
        layer_kernel, "layer",
        (*weight_pieces, m0, m1, m2, turned_grad, rotor_rows, edge_bias[0], targets[:, None], live[:, None],
         w_alpha, place[None], *positions),
        [((4 * TERM_ROWS, CH), BF16)] * 8 + [((160, MCOEF * CH), BF16), ((160, MCOEF * CH), BF16)],
        [((1536, 640), BF16), ((1024, 1024), BF16), ((1024, 768), BF16), ((160, MCOEF * CH), BF16),
         ((160, 640), BF16), ((320, 1024), BF16), ((320, 768), BF16),
         ((160, 1536), BF16), ((320, 1024), BF16), ((320, 1024), BF16),
         ((160, 1280), BF16), ((320, 1024), BF16), ((320, 768), BF16), ((160, FULL), BF16)],
        5_000_000_000, 160 * 136,
    )
    term_pieces, (scaled, grad_dst) = outs[:8], outs[8:]
    node_out, grad_local = call(
        nodes_kernel, "nodes", (rotor_rows, scaled, grad_dst, targets[None]),
        [((4, FULL), BF16), ((4, FULL), F32)], [((160, FULL), BF16), ((160, FULL), BF16)],
        600_000_000,
    )
    terms, shard, (node_out, grad_local) = scatter_sum(term_pieces, (node_out, grad_local))
    grad_remote = terms.transpose(1, 0, 2).reshape(4, FULL)
    shard = shard.transpose(1, 0, 2).reshape(10, 640)
    n_rep = lax.axis_size("rep")
    copies = lax.all_to_all(jnp.broadcast_to(shard, (n_rep, 10, 640)), "rep", split_axis=0, concat_axis=0, tiled=True)
    grad_w0 = jnp.sum(copies, axis=0)
    return node_out[None], (grad_local + grad_remote)[None], grad_w0


def solution(mesh):
    placed = (
        P("rep", "edge", None), P("rep", "edge", None), P("rep", "edge", None), P("rep", "edge"),
        P("rep", "edge"), P("rep", "edge"), P("rep", "edge", None), P("edge", None),
        P(None, "edge", None), P(None, "edge", None), P(), P("rep", "edge", None),
    )
    return jax.shard_map(
        local, mesh=mesh, in_specs=placed,
        out_specs=(P("rep", "edge", None), P("rep", "edge", None), P("edge", None)),
        check_vma=False,
    )
```

```python
import jax
import jax.numpy as jnp
import numpy as np
from jax import lax
from jax.experimental import pallas as pl
from jax.experimental.pallas import tpu as pltpu
from jax.sharding import PartitionSpec as P

LCOEF = 25
MCOEF = 19
CH = 128
HEADS = 8
EDGES = 160
BLOCK = 16
NZ, NX = 16, 4
FULL = LCOEF * CH
ROWS_OF = {0: (0,), 1: (1, 5, 9), 2: (2, 6, 10, 13, 16), 3: (3, 7, 11, 14, 17), 4: (4, 8, 12, 15, 18)}
NEAR = (0, 1, 2, -1)
FAR_ROWS = 400
DEPTHS = (48, 32, 32)
UNITS = (5, 8, 6)
WEIGHT_ROWS = 240 + 256 + 192
TERM_ROWS = 400 + 240
INVERSE_AT, POSITION_AT = (0, 1536, 2560), (3584, 4864, 5888)
VMEM_LIMIT = 56 * 2**20
F32, BF16 = jnp.float32, jnp.bfloat16


def where_to(i, dz, dx, dc):
    z, x, c = i // 8, (i // 2) % 4, i % 2
    sign = 1 - 2 * c
    return ((z + sign * dz) % NZ) * 8 + ((x + dx) % NX) * 2 + (c + dc) % 2


def pull(a, dz=0, dx=0, dc=0):
    return lax.ppermute(a, "edge", [(where_to(i, dz, dx, dc), i) for i in range(128)])


def push(a, dz=0, dx=0, dc=0):
    return lax.ppermute(a, "edge", [(i, where_to(i, dz, dx, dc)) for i in range(128)])


def block_place(owner, me):
    sign = 1 - 2 * (owner % 2)
    jz = (sign * (owner // 8 - me // 8) + 1) % NZ
    xr = ((owner // 2) % 4 - (me // 2) % 4) % NX
    cr = (owner % 2 + me % 2) % 2
    near = (jz % 4 + 3) % 4
    return cr * 16 + xr * 4 + near, jz // 4


def block_owner(place, far, me):
    cr, xr, near = place // 16, (place // 4) % 4, place % 4
    sign = 1 - 2 * ((me + cr) % 2)
    offset = (near + 1) % 4 - 1
    z = (me // 8 + sign * (4 * far + offset)) % NZ
    x = ((me // 2) % 4 + xr) % NX
    return z * 8 + x * 2 + (me % 2 + cr) % 2


def x_pieces(block):
    return (block,) + tuple(pull(block, dx=x) for x in (1, 2, 3))


def scatter_sum(pieces, beside):
    def add(a, *more):
        total = a.astype(F32)
        for m in more:
            total = total + m.astype(F32)
        return total

    a = [add(pieces[x], push(pieces[4 + x], dc=1)).astype(BF16) for x in range(4)]
    arrived, beside = lax.optimization_barrier(([push(a[x], dx=x) for x in (2, 1, 3)], beside))
    total = add(a[0], *arrived).astype(BF16)
    parts = [total[n * TERM_ROWS : (n + 1) * TERM_ROWS] for n in range(4)]
    total = add(parts[0], *(push(parts[n], dz=NEAR[n]) for n in (1, 2, 3))).astype(BF16)
    terms, shard = total[:400].reshape(25, 16, CH), total[400:].reshape(5, 48, CH)

    def part(n):
        return jnp.concatenate(
            [terms[:, 4 * n : 4 * n + 4].reshape(100, CH), shard[:, 10 * n : 10 * n + 10].reshape(50, CH)], axis=0
        )

    total = add(part(0), *(push(part(n), dz=4 * n) for n in (1, 2, 3)))
    return total[:100].reshape(25, 4, CH), total[100:].reshape(5, 10, CH), beside


def hot(index, shape, axis):
    return jnp.where(index == lax.broadcasted_iota(jnp.int32, shape, axis), F32(1), F32(0)).astype(BF16)


def mm(a, b):
    return jnp.dot(a, b, preferred_element_type=F32)


def mm_nt(a, b):
    return lax.dot_general(a, b, (((1,), (1,)), ((), ())), preferred_element_type=F32)


def mm_tn(a, b, precision=None):
    return lax.dot_general(a, b, (((0,), (0,)), ((), ())), precision=precision, preferred_element_type=F32)


def frame_slot(row):
    if row < 5:
        return 0, 0, row
    if row < 13:
        return 1, ((row - 5) // 4) * EDGES, (row - 5) % 4
    return 2, ((row - 13) // 3) * EDGES, (row - 13) % 3


def rotate_kernel(*refs):
    pieces = refs[:8]
    rot, edge_rows, local, maps = refs[8:12]
    m0, m1, m2, turned_grad = refs[12:16]
    feats, srcf, dstf, gradf, n0, n1, n2 = refs[16:]
    for k, piece in enumerate(pieces):
        for near in range(4):
            row = k * 64 + near * 16
            for u in range(LCOEF):
                at = near * FAR_ROWS + u * 16
                feats[row : row + 16, u * CH : (u + 1) * CH] = piece[at : at + 16, :]
    source_hot = hot(edge_rows[0:1, :], (512, EDGES), 0)
    t = edge_rows[1:2, :]
    rows = lax.broadcasted_iota(jnp.int32, (16, EDGES), 0)
    feat_hot = jnp.where(rows == t, F32(1), F32(0)).astype(BF16)
    grad_hot = jnp.where((rows == t + 4) | (rows == t + 8), F32(1), F32(0)).astype(BF16)
    for first in range(0, FULL, 640):
        cut = slice(first, first + 640)
        srcf[:, cut] = mm_tn(source_hot, feats[:, cut]).astype(BF16)
        dstf[:, cut] = mm_tn(feat_hot, local[:, cut]).astype(BF16)
        gradf[:, cut] = mm_tn(grad_hot, local[:, cut])

    stacked = (n0, n1, n2)

    def turn(step, carry):
        e0 = pl.multiple_of(step * BLOCK, BLOCK)
        rows_here = pl.ds(e0, BLOCK)
        rotors = rot[rows_here, :].astype(F32)
        for degree, rows in ROWS_OF.items():
            sums = [None] * len(rows)
            for col in range(degree * degree, (degree + 1) ** 2):
                cut = slice(col * CH, (col + 1) * CH)
                s, d, g = srcf[rows_here, cut].astype(F32), dstf[rows_here, cut].astype(F32), gradf[rows_here, cut]
                for n, row in enumerate(rows):
                    r = jnp.broadcast_to(rotors[:, row * LCOEF + col : row * LCOEF + col + 1], (BLOCK, CH))
                    terms = (r * s, r * d, r * g)
                    sums[n] = terms if sums[n] is None else tuple(a + b for a, b in zip(sums[n], terms))
            for n, row in enumerate(rows):
                array, base, column = frame_slot(row)
                out = stacked[array]
                out_rows = pl.ds(pl.multiple_of(base + e0, BLOCK), BLOCK)
                out[out_rows, column * 256 : column * 256 + CH] = sums[n][0].astype(BF16)
                out[out_rows, column * 256 + CH : column * 256 + 256] = sums[n][1].astype(BF16)
                turned_grad[rows_here, row * CH : (row + 1) * CH] = sums[n][2]
        return carry

    lax.fori_loop(0, EDGES // BLOCK, turn, 0)
    for natural, ordered, start in ((n0, m0, INVERSE_AT[0]), (n1, m1, INVERSE_AT[1]), (n2, m2, INVERSE_AT[2])):
        depth = natural.shape[1]
        for first in range(0, ordered.shape[1], 256):
            inverse = maps[:, start + first : start + first + 256]
            ordered[:, first : first + 256] = mm(natural[...], hot(inverse, (depth, 256), 0)).astype(BF16)


def layer_kernel(*refs):
    pieces = refs[:8]
    m0, m1, m2, turned_grad, rot, bias, alpha_ref, edge_rows, maps = refs[8:17]
    terms_out = refs[17:25]
    scaled_out, grad_dst = refs[25:27]
    w0, w1, w2, values, d0, d1, d2, p0, p1, p2, g0, g1, g2, src_terms = refs[27:]
    for k, piece in enumerate(pieces):
        for near in range(4):
            at = near * WEIGHT_ROWS
            for out, units, rows in zip((w0, w1, w2), UNITS, DEPTHS):
                to = (k * 4 + near) * rows
                for u in range(units):
                    out[to : to + rows, u * CH : (u + 1) * CH] = piece[at : at + rows, :]
                    at += rows
    z0 = mm(m0[...], w0[...])
    for row in range(5):
        values[:, row * CH : (row + 1) * CH] = z0[:, row * CH : (row + 1) * CH].astype(BF16)
    z1 = mm(m1[...], w1[...])
    values[:, 5 * CH : 9 * CH] = (z1[:EDGES, :512] - z1[EDGES:, 512:]).astype(BF16)
    values[:, 9 * CH : 13 * CH] = (z1[EDGES:, :512] + z1[:EDGES, 512:]).astype(BF16)
    z2 = mm(m2[...], w2[...])
    values[:, 13 * CH : 16 * CH] = (z2[:EDGES, :384] - z2[EDGES:, 384:]).astype(BF16)
    values[:, 16 * CH : 19 * CH] = (z2[EDGES:, :384] + z2[:EDGES, 384:]).astype(BF16)

    v = z0[:, :CH]
    sigma = 1.0 / (1.0 + jnp.exp(-v))
    alpha = alpha_ref[...]
    logits = bias[...] + mm_nt(alpha, (v * sigma).astype(BF16))
    t = edge_rows[1:2, :]
    live = edge_rows[2:3, :] > 0
    members = [live & (t == n) for n in range(4)]

    def over_targets(array, empty, reduce):
        result = jnp.zeros((HEADS, EDGES), F32)
        for member in members:
            one = reduce(jnp.where(member, array, F32(empty)), axis=1, keepdims=True)
            result = jnp.where(member, one, result)
        return result

    top = over_targets(logits, -1e30, jnp.max)
    expo = jnp.where(live, jnp.exp(jnp.where(live, logits - top, F32(0))), F32(0))
    denom = jnp.where(live, over_targets(expo, 0.0, jnp.sum), F32(1))
    attn = expo / denom
    head_of = (
        lax.broadcasted_iota(jnp.int32, (HEADS, CH), 1) // (CH // HEADS)
        == lax.broadcasted_iota(jnp.int32, (HEADS, CH), 0)
    )
    spread = jnp.where(head_of, F32(1), F32(0))
    scale = mm_tn(attn, spread, lax.Precision.HIGHEST)
    dscale = jnp.zeros((EDGES, CH), F32)
    for row in range(MCOEF):
        cut = slice(row * CH, (row + 1) * CH)
        value = values[:, cut].astype(F32)
        dscale = dscale + turned_grad[:, cut] * value
        scaled_out[:, cut] = (scale * value).astype(BF16)
    dattn = lax.dot_general(
        spread, dscale, (((1,), (1,)), ((), ())), precision=lax.Precision.HIGHEST, preferred_element_type=F32
    )
    dlogits = attn * (dattn - over_targets(attn * dattn, 0.0, jnp.sum))
    dscalars = mm_tn(dlogits, alpha.astype(F32), lax.Precision.HIGHEST).astype(BF16).astype(F32)
    dv = dscalars * (sigma * (1.0 + v * (1.0 - sigma)))
    for row in range(MCOEF):
        cut = slice(row * CH, (row + 1) * CH)
        dvalue = (scale * turned_grad[:, cut]).astype(BF16)
        if row == 0:
            dvalue = (dvalue.astype(F32) + dv).astype(BF16)
        if row < 5:
            d0[:, cut] = dvalue
            continue
        out, width, column, plus = (d1, 512, (row - 5) % 4, row < 9) if row < 13 else (d2, 384, (row - 13) % 3, row < 16)
        a, b = column * CH, width + column * CH
        if plus:
            out[:EDGES, a : a + CH] = dvalue
            out[EDGES:, b : b + CH] = -dvalue
        else:
            out[EDGES:, a : a + CH] = dvalue
            out[:EDGES, b : b + CH] = dvalue
    dw = lax.dot_general(m0[...], d0[...], (((0,), (0,)), ((), ())), preferred_element_type=F32)
    for k in range(8):
        for near in range(4):
            row = (k * 4 + near) * 48
            for u in range(5):
                at = near * TERM_ROWS + 400 + u * 48
                terms_out[k][at : at + 48, :] = dw[row : row + 48, u * CH : (u + 1) * CH].astype(BF16)
    for d, w, p, g, start in zip((d0, d1, d2), (w0, w1, w2), (p0, p1, p2), (g0, g1, g2), POSITION_AT):
        p[...] = mm_nt(d[...], w[...]).astype(BF16)
        for first in range(0, g.shape[1], 256):
            position = maps[:, start + first : start + first + 256]
            g[:, first : first + 256] = mm(p[...], hot(position, (w.shape[0], 256), 0)).astype(BF16)
    stacked = (g0, g1, g2)
    for row in range(MCOEF):
        array, base, column = frame_slot(row)
        grad_dst[:, row * CH : (row + 1) * CH] = stacked[array][base : base + EDGES, column * 256 + CH : column * 256 + 256]

    def turn(step, carry):
        e0 = pl.multiple_of(step * BLOCK, BLOCK)
        rows_here = pl.ds(e0, BLOCK)
        rotors = rot[rows_here, :].astype(F32)
        for degree, rows in ROWS_OF.items():
            first = degree * degree
            sums = [None] * (2 * degree + 1)
            for row in rows:
                array, base, column = frame_slot(row)
                s = stacked[array][pl.ds(pl.multiple_of(base + e0, BLOCK), BLOCK), column * 256 : column * 256 + CH]
                s = s.astype(F32)
                for n in range(2 * degree + 1):
                    at = row * LCOEF + first + n
                    term = jnp.broadcast_to(rotors[:, at : at + 1], (BLOCK, CH)) * s
                    sums[n] = term if sums[n] is None else sums[n] + term
            for n in range(2 * degree + 1):
                src_terms[rows_here, (first + n) * CH : (first + n + 1) * CH] = sums[n].astype(BF16)
        return carry

    lax.fori_loop(0, EDGES // BLOCK, turn, 0)
    chosen = hot(edge_rows[0:1, :], (512, EDGES), 0)
    for first in range(0, FULL, 640):
        block = mm(chosen, src_terms[:, first : first + 640]).astype(BF16)
        for k in range(8):
            for near in range(4):
                row = k * 64 + near * 16
                for n in range(5):
                    at = near * TERM_ROWS + (first // CH + n) * 16
                    terms_out[k][at : at + 16, :] = block[row : row + 16, n * CH : (n + 1) * CH]


def nodes_kernel(rot, scaled, grad_dst, edge_rows, node_out, grad_local, back, terms):
    def turn(step, carry):
        e0 = pl.multiple_of(step * BLOCK, BLOCK)
        rows_here = pl.ds(e0, BLOCK)
        rotors = rot[rows_here, :].astype(F32)
        for degree, rows in ROWS_OF.items():
            first = degree * degree
            sums = [None] * (2 * degree + 1)
            for row in rows:
                a = scaled[rows_here, row * CH : (row + 1) * CH].astype(F32)
                b = grad_dst[rows_here, row * CH : (row + 1) * CH].astype(F32)
                for n in range(2 * degree + 1):
                    at = row * LCOEF + first + n
                    r = jnp.broadcast_to(rotors[:, at : at + 1], (BLOCK, CH))
                    sums[n] = (r * a, r * b) if sums[n] is None else (sums[n][0] + r * a, sums[n][1] + r * b)
            for n in range(2 * degree + 1):
                cut = slice((first + n) * CH, (first + n + 1) * CH)
                back[rows_here, cut] = sums[n][0].astype(BF16)
                terms[rows_here, cut] = sums[n][1].astype(BF16)
        return carry

    lax.fori_loop(0, EDGES // BLOCK, turn, 0)
    chosen = hot(edge_rows[1:2, :], (16, EDGES), 0)
    for first in range(0, FULL, 640):
        cut = slice(first, first + 640)
        node_out[:, cut] = mm(chosen, back[:, cut])[:4].astype(BF16)
        grad_local[:, cut] = mm(chosen, terms[:, cut])[:4]


def call(kernel, name, args, outs, scratch, flops, transcendentals=0):
    moved = sum(a.size * a.dtype.itemsize for a in args)
    return pl.pallas_call(
        kernel,
        out_shape=tuple(jax.ShapeDtypeStruct(s, t) for s, t in outs),
        in_specs=[pl.BlockSpec(memory_space=pltpu.VMEM)] * len(args),
        out_specs=tuple(pl.BlockSpec(memory_space=pltpu.VMEM) for _ in outs),
        scratch_shapes=[pltpu.VMEM(s, t) for s, t in scratch],
        compiler_params=pltpu.CompilerParams(vmem_limit_bytes=VMEM_LIMIT),
        cost_estimate=pl.CostEstimate(flops=flops, bytes_accessed=moved, transcendentals=transcendentals),
        name=name,
    )(*args)


def units_of(array):
    rows, width = array.shape
    return array.reshape(rows, width // CH, CH).transpose(1, 0, 2).reshape(-1, CH)


def index_maps(me):
    inverse, position = [], []
    for rows, depth in zip((10, 8, 6), DEPTHS):
        p = np.arange(32 * depth)
        inside = p % depth
        inverse.append((p // depth, np.minimum(inside // rows, 3), np.full_like(p, rows), inside % rows, inside < 4 * rows))
        k = np.arange(128 * rows)
        position.append((k // rows, np.full_like(k, depth), np.full_like(k, rows), k % rows))
    place, far, rows, rest, inside = (jnp.asarray(np.concatenate(a), jnp.int32) for a in zip(*inverse))
    natural = jnp.where(inside > 0, block_owner(place, far, me) * rows + rest, -1)
    owner, depth, rows, rest = (jnp.asarray(np.concatenate(a), jnp.int32) for a in zip(*position))
    block, far = block_place(owner, me)
    return jnp.concatenate([natural, block * depth + far * rows + rest])[None]


def local(
    node_feat, rotation, source_owner, source_row, target_row, live_count, edge_bias,
    w_m0, w_m1, w_m2, w_alpha, out_grad,
):
    me = lax.axis_index("edge")
    features = node_feat[0]
    rotor_rows = rotation[0]
    live = (jnp.arange(EDGES, dtype=jnp.int32) < live_count[0, 0]).astype(jnp.int32)
    block, far = block_place(source_owner[0, :, 0], me)
    edge_rows = jnp.stack([block * 16 + far * 4 + source_row[0], target_row[0], live], axis=0)

    w1 = jnp.concatenate([w_m1[0], w_m1[1]], axis=1)
    w2 = jnp.concatenate([w_m2[0], w_m2[1]], axis=1)
    shards = (features, w_m0, w1, w2)
    own = jnp.concatenate([units_of(a) for a in shards], axis=0)
    blocks = [own] + [pull(own, dz=4 * a) for a in (1, 2, 3)]
    merged, at = [], 0
    for shard, depth in zip(shards, (16,) + DEPTHS):
        rows, units = shard.shape[0], shard.shape[1] // CH
        parts = [b[at : at + units * rows].reshape(units, rows, CH) for b in blocks]
        if depth > 4 * rows:
            parts.append(jnp.zeros((units, depth - 4 * rows, CH), BF16))
        merged.append(jnp.concatenate(parts, axis=1).reshape(units * depth, CH))
        at += units * rows
    far_block = jnp.concatenate(merged, axis=0)
    blocks = [far_block] + [pull(far_block, dz=NEAR[n]) for n in (1, 2, 3)]
    feature_x = x_pieces(jnp.concatenate([b[:FAR_ROWS] for b in blocks], axis=0))
    weight_x = x_pieces(jnp.concatenate([b[FAR_ROWS:] for b in blocks], axis=0))
    feature_pieces = feature_x + tuple(pull(a, dc=1) for a in feature_x)

    maps = index_maps(me)
    cotangent = out_grad[0]
    high = lax.reduce_precision(cotangent, 8, 7)
    own_rows = jnp.concatenate(
        [features, high.astype(BF16), (cotangent - high).astype(BF16), jnp.zeros((4, FULL), BF16)], axis=0
    )

    m0, m1, m2, turned_grad = call(
        rotate_kernel, "rotate",
        (*feature_pieces, rotor_rows, edge_rows, own_rows, maps),
        [((160, 1536), BF16), ((320, 1024), BF16), ((320, 1024), BF16), ((160, MCOEF * CH), F32)],
        [((512, FULL), BF16), ((160, FULL), BF16), ((160, FULL), BF16), ((160, FULL), F32),
         ((160, 1280), BF16), ((320, 1024), BF16), ((320, 768), BF16)],
        3_000_000_000,
    )
    others = [lax.optimization_barrier((m0, weight_x[x]))[1] for x in (1, 2, 3)]
    weight_x = (weight_x[0], *others)
    weight_pieces = weight_x + tuple(pull(a, dc=1) for a in weight_x)
    outs = call(
        layer_kernel, "layer",
        (*weight_pieces, m0, m1, m2, turned_grad, rotor_rows, edge_bias[0].T, w_alpha.T, edge_rows, maps),
        [((4 * TERM_ROWS, CH), BF16)] * 8 + [((160, MCOEF * CH), BF16), ((160, MCOEF * CH), BF16)],
        [((1536, 640), BF16), ((1024, 1024), BF16), ((1024, 768), BF16), ((160, MCOEF * CH), BF16),
         ((160, 640), BF16), ((320, 1024), BF16), ((320, 768), BF16),
         ((160, 1536), BF16), ((320, 1024), BF16), ((320, 1024), BF16),
         ((160, 1280), BF16), ((320, 1024), BF16), ((320, 768), BF16), ((160, FULL), BF16)],
        5_000_000_000, 160 * 136,
    )
    term_pieces, (scaled, grad_dst) = outs[:8], outs[8:]
    node_out, grad_local = call(
        nodes_kernel, "nodes", (rotor_rows, scaled, grad_dst, edge_rows),
        [((4, FULL), BF16), ((4, FULL), F32)], [((160, FULL), BF16), ((160, FULL), BF16)],
        600_000_000,
    )
    terms, shard, (node_out, grad_local) = scatter_sum(term_pieces, (node_out, grad_local))
    grad_remote = terms.transpose(1, 0, 2).reshape(4, FULL)
    shard = shard.transpose(1, 0, 2).reshape(10, 640)
    n_rep = lax.axis_size("rep")
    copies = lax.all_to_all(jnp.broadcast_to(shard, (n_rep, 10, 640)), "rep", split_axis=0, concat_axis=0, tiled=True)
    grad_w0 = jnp.sum(copies, axis=0)
    return node_out[None], (grad_local + grad_remote)[None], grad_w0


def solution(mesh):
    placed = (
        P("rep", "edge", None), P("rep", "edge", None), P("rep", "edge", None), P("rep", "edge"),
        P("rep", "edge"), P("rep", "edge"), P("rep", "edge", None), P("edge", None),
        P(None, "edge", None), P(None, "edge", None), P(), P("rep", "edge", None),
    )
    return jax.shard_map(
        local, mesh=mesh, in_specs=placed,
        out_specs=(P("rep", "edge", None), P("rep", "edge", None), P("edge", None)),
        check_vma=False,
    )
```

```python
import jax
import jax.numpy as jnp
import numpy as np
from jax import lax
from jax.experimental import pallas as pl
from jax.experimental.pallas import tpu as pltpu
from jax.sharding import PartitionSpec as P

LCOEF = 25
MCOEF = 19
CH = 128
HEADS = 8
EDGES = 160
BLOCK = 16
NZ, NX = 16, 4
FULL = LCOEF * CH
ROWS_OF = {0: (0,), 1: (1, 5, 9), 2: (2, 6, 10, 13, 16), 3: (3, 7, 11, 14, 17), 4: (4, 8, 12, 15, 18)}
NEAR = (0, 1, 2, -1)
FAR_ROWS = 400
DEPTHS = (40, 32, 24)
UNITS = (5, 8, 6)
TERM_ROWS = 400 + 240
INVERSE_AT, POSITION_AT = (0, 1280, 2304), (3072, 4352, 5376)
VMEM_LIMIT = 56 * 2**20
F32, BF16 = jnp.float32, jnp.bfloat16


def where_to(i, dz, dx, dc):
    z, x, c = i // 8, (i // 2) % 4, i % 2
    sign = 1 - 2 * c
    return ((z + sign * dz) % NZ) * 8 + ((x + dx) % NX) * 2 + (c + dc) % 2


def pull(a, dz=0, dx=0, dc=0):
    return lax.ppermute(a, "edge", [(where_to(i, dz, dx, dc), i) for i in range(128)])


def push(a, dz=0, dx=0, dc=0):
    return lax.ppermute(a, "edge", [(i, where_to(i, dz, dx, dc)) for i in range(128)])


def block_place(owner, me):
    sign = 1 - 2 * (owner % 2)
    jz = (sign * (owner // 8 - me // 8) + 1) % NZ
    xr = ((owner // 2) % 4 - (me // 2) % 4) % NX
    cr = (owner % 2 + me % 2) % 2
    near = (jz % 4 + 3) % 4
    return cr * 16 + xr * 4 + near, jz // 4


def block_owner(place, far, me):
    cr, xr, near = place // 16, (place // 4) % 4, place % 4
    sign = 1 - 2 * ((me + cr) % 2)
    offset = (near + 1) % 4 - 1
    z = (me // 8 + sign * (4 * far + offset)) % NZ
    x = ((me // 2) % 4 + xr) % NX
    return z * 8 + x * 2 + (me % 2 + cr) % 2


def x_pieces(block):
    return (block,) + tuple(pull(block, dx=x) for x in (1, 2, 3))


def scatter_sum(pieces, beside):
    def add(a, *more):
        total = a.astype(F32)
        for m in more:
            total = total + m.astype(F32)
        return total

    a = [add(pieces[x], push(pieces[4 + x], dc=1)).astype(BF16) for x in range(4)]
    arrived, beside = lax.optimization_barrier(([push(a[x], dx=x) for x in (2, 1, 3)], beside))
    total = add(a[0], *arrived).astype(BF16)
    parts = [total[n * TERM_ROWS : (n + 1) * TERM_ROWS] for n in range(4)]
    total = add(parts[0], *(push(parts[n], dz=NEAR[n]) for n in (1, 2, 3))).astype(BF16)
    terms, shard = total[:400].reshape(25, 16, CH), total[400:].reshape(5, 48, CH)

    def part(n):
        return jnp.concatenate(
            [terms[:, 4 * n : 4 * n + 4].reshape(100, CH), shard[:, 10 * n : 10 * n + 10].reshape(50, CH)], axis=0
        )

    total = add(part(0), *(push(part(n), dz=4 * n) for n in (1, 2, 3)))
    return total[:100].reshape(25, 4, CH), total[100:].reshape(5, 10, CH), beside


def hot(index, shape, axis):
    return jnp.where(index == lax.broadcasted_iota(jnp.int32, shape, axis), F32(1), F32(0)).astype(BF16)


def mm(a, b):
    return jnp.dot(a, b, preferred_element_type=F32)


def mm_nt(a, b):
    return lax.dot_general(a, b, (((1,), (1,)), ((), ())), preferred_element_type=F32)


def mm_tn(a, b, precision=None):
    return lax.dot_general(a, b, (((0,), (0,)), ((), ())), precision=precision, preferred_element_type=F32)


def frame_slot(row):
    if row < 5:
        return 0, 0, row
    if row < 13:
        return 1, ((row - 5) // 4) * EDGES, (row - 5) % 4
    return 2, ((row - 13) // 3) * EDGES, (row - 13) % 3


def rotate_kernel(*refs):
    pieces = refs[:8]
    rot, edge_rows, local, maps = refs[8:12]
    m0, m1, m2, turned_grad = refs[12:16]
    feats, srcf, dstf, gradf, n0, n1, n2 = refs[16:]
    for k, piece in enumerate(pieces):
        for near in range(4):
            row = k * 64 + near * 16
            for u in range(LCOEF):
                at = near * FAR_ROWS + u * 16
                feats[row : row + 16, u * CH : (u + 1) * CH] = piece[at : at + 16, :]
    source_hot = hot(edge_rows[0:1, :], (512, EDGES), 0)
    t = edge_rows[1:2, :]
    rows = lax.broadcasted_iota(jnp.int32, (16, EDGES), 0)
    feat_hot = jnp.where(rows == t, F32(1), F32(0)).astype(BF16)
    grad_hot = jnp.where((rows == t + 4) | (rows == t + 8), F32(1), F32(0)).astype(BF16)
    for first in range(0, FULL, 640):
        cut = slice(first, first + 640)
        srcf[:, cut] = mm_tn(source_hot, feats[:, cut]).astype(BF16)
        dstf[:, cut] = mm_tn(feat_hot, local[:, cut]).astype(BF16)
        gradf[:, cut] = mm_tn(grad_hot, local[:, cut])

    stacked = (n0, n1, n2)

    def turn(step, carry):
        e0 = pl.multiple_of(step * BLOCK, BLOCK)
        rows_here = pl.ds(e0, BLOCK)
        rotors = rot[rows_here, :].astype(F32)
        for degree, rows in ROWS_OF.items():
            sums = [None] * len(rows)
            for col in range(degree * degree, (degree + 1) ** 2):
                cut = slice(col * CH, (col + 1) * CH)
                s, d, g = srcf[rows_here, cut].astype(F32), dstf[rows_here, cut].astype(F32), gradf[rows_here, cut]
                for n, row in enumerate(rows):
                    r = jnp.broadcast_to(rotors[:, row * LCOEF + col : row * LCOEF + col + 1], (BLOCK, CH))
                    terms = (r * s, r * d, r * g)
                    sums[n] = terms if sums[n] is None else tuple(a + b for a, b in zip(sums[n], terms))
            for n, row in enumerate(rows):
                array, base, column = frame_slot(row)
                out = stacked[array]
                out_rows = pl.ds(pl.multiple_of(base + e0, BLOCK), BLOCK)
                out[out_rows, column * 256 : column * 256 + CH] = sums[n][0].astype(BF16)
                out[out_rows, column * 256 + CH : column * 256 + 256] = sums[n][1].astype(BF16)
                turned_grad[rows_here, row * CH : (row + 1) * CH] = sums[n][2]
        return carry

    lax.fori_loop(0, EDGES // BLOCK, turn, 0)
    for natural, ordered, start in ((n0, m0, INVERSE_AT[0]), (n1, m1, INVERSE_AT[1]), (n2, m2, INVERSE_AT[2])):
        depth = natural.shape[1]
        for first in range(0, ordered.shape[1], 256):
            inverse = maps[:, start + first : start + first + 256]
            ordered[:, first : first + 256] = mm(natural[...], hot(inverse, (depth, 256), 0)).astype(BF16)


def layer_kernel(*refs):
    pieces = refs[:8]
    m0, m1, m2, turned_grad, rot, bias, alpha_ref, edge_rows, maps = refs[8:17]
    terms_out = refs[17:25]
    scaled_out, grad_dst = refs[25:27]
    w0, w1, w2, values, d0, d1, d2, p0, p1, p2, g0, g1, g2, src_terms = refs[27:]
    for k, piece in enumerate(pieces):
        at = 0
        for out, units, depth in zip((w0, w1, w2), UNITS, DEPTHS):
            rows = 4 * depth
            for u in range(units):
                out[k * rows : (k + 1) * rows, u * CH : (u + 1) * CH] = piece[at : at + rows, :]
                at += rows
    z0 = mm(m0[...], w0[...])
    for row in range(5):
        values[:, row * CH : (row + 1) * CH] = z0[:, row * CH : (row + 1) * CH].astype(BF16)
    z1 = mm(m1[...], w1[...])
    values[:, 5 * CH : 9 * CH] = (z1[:EDGES, :512] - z1[EDGES:, 512:]).astype(BF16)
    values[:, 9 * CH : 13 * CH] = (z1[EDGES:, :512] + z1[:EDGES, 512:]).astype(BF16)
    z2 = mm(m2[...], w2[...])
    values[:, 13 * CH : 16 * CH] = (z2[:EDGES, :384] - z2[EDGES:, 384:]).astype(BF16)
    values[:, 16 * CH : 19 * CH] = (z2[EDGES:, :384] + z2[:EDGES, 384:]).astype(BF16)

    v = z0[:, :CH]
    sigma = 1.0 / (1.0 + jnp.exp(-v))
    alpha = alpha_ref[...]
    logits = bias[...] + mm_nt(alpha, (v * sigma).astype(BF16))
    t = edge_rows[1:2, :]
    live = edge_rows[2:3, :] > 0
    members = [live & (t == n) for n in range(4)]

    def over_targets(array, empty, reduce):
        result = jnp.zeros((HEADS, EDGES), F32)
        for member in members:
            one = reduce(jnp.where(member, array, F32(empty)), axis=1, keepdims=True)
            result = jnp.where(member, one, result)
        return result

    top = over_targets(logits, -1e30, jnp.max)
    expo = jnp.where(live, jnp.exp(jnp.where(live, logits - top, F32(0))), F32(0))
    denom = jnp.where(live, over_targets(expo, 0.0, jnp.sum), F32(1))
    attn = expo / denom
    head_of = (
        lax.broadcasted_iota(jnp.int32, (HEADS, CH), 1) // (CH // HEADS)
        == lax.broadcasted_iota(jnp.int32, (HEADS, CH), 0)
    )
    spread = jnp.where(head_of, F32(1), F32(0))
    scale = mm_tn(attn, spread, lax.Precision.HIGHEST)
    dscale = jnp.zeros((EDGES, CH), F32)
    for row in range(MCOEF):
        cut = slice(row * CH, (row + 1) * CH)
        value = values[:, cut].astype(F32)
        dscale = dscale + turned_grad[:, cut] * value
        scaled_out[:, cut] = (scale * value).astype(BF16)
    dattn = lax.dot_general(
        spread, dscale, (((1,), (1,)), ((), ())), precision=lax.Precision.HIGHEST, preferred_element_type=F32
    )
    dlogits = attn * (dattn - over_targets(attn * dattn, 0.0, jnp.sum))
    dscalars = mm_tn(dlogits, alpha.astype(F32), lax.Precision.HIGHEST).astype(BF16).astype(F32)
    dv = dscalars * (sigma * (1.0 + v * (1.0 - sigma)))
    for row in range(MCOEF):
        cut = slice(row * CH, (row + 1) * CH)
        dvalue = (scale * turned_grad[:, cut]).astype(BF16)
        if row == 0:
            dvalue = (dvalue.astype(F32) + dv).astype(BF16)
        if row < 5:
            d0[:, cut] = dvalue
            continue
        out, width, column, plus = (d1, 512, (row - 5) % 4, row < 9) if row < 13 else (d2, 384, (row - 13) % 3, row < 16)
        a, b = column * CH, width + column * CH
        if plus:
            out[:EDGES, a : a + CH] = dvalue
            out[EDGES:, b : b + CH] = -dvalue
        else:
            out[EDGES:, a : a + CH] = dvalue
            out[:EDGES, b : b + CH] = dvalue
    dw = lax.dot_general(m0[...], d0[...], (((0,), (0,)), ((), ())), preferred_element_type=F32)
    for k in range(8):
        for near in range(4):
            row = (k * 4 + near) * 40
            for u in range(5):
                at = near * TERM_ROWS + 400 + u * 48
                rows = jnp.concatenate([dw[row : row + 40, u * CH : (u + 1) * CH], jnp.zeros((8, CH), F32)], axis=0)
                terms_out[k][at : at + 48, :] = rows.astype(BF16)
    for d, w, p, g, start in zip((d0, d1, d2), (w0, w1, w2), (p0, p1, p2), (g0, g1, g2), POSITION_AT):
        p[...] = mm_nt(d[...], w[...]).astype(BF16)
        for first in range(0, g.shape[1], 256):
            position = maps[:, start + first : start + first + 256]
            g[:, first : first + 256] = mm(p[...], hot(position, (w.shape[0], 256), 0)).astype(BF16)
    stacked = (g0, g1, g2)
    for row in range(MCOEF):
        array, base, column = frame_slot(row)
        grad_dst[:, row * CH : (row + 1) * CH] = stacked[array][base : base + EDGES, column * 256 + CH : column * 256 + 256]

    def turn(step, carry):
        e0 = pl.multiple_of(step * BLOCK, BLOCK)
        rows_here = pl.ds(e0, BLOCK)
        rotors = rot[rows_here, :].astype(F32)
        for degree, rows in ROWS_OF.items():
            first = degree * degree
            sums = [None] * (2 * degree + 1)
            for row in rows:
                array, base, column = frame_slot(row)
                s = stacked[array][pl.ds(pl.multiple_of(base + e0, BLOCK), BLOCK), column * 256 : column * 256 + CH]
                s = s.astype(F32)
                for n in range(2 * degree + 1):
                    at = row * LCOEF + first + n
                    term = jnp.broadcast_to(rotors[:, at : at + 1], (BLOCK, CH)) * s
                    sums[n] = term if sums[n] is None else sums[n] + term
            for n in range(2 * degree + 1):
                src_terms[rows_here, (first + n) * CH : (first + n + 1) * CH] = sums[n].astype(BF16)
        return carry

    lax.fori_loop(0, EDGES // BLOCK, turn, 0)
    chosen = hot(edge_rows[0:1, :], (512, EDGES), 0)
    for first in range(0, FULL, 640):
        block = mm(chosen, src_terms[:, first : first + 640]).astype(BF16)
        for k in range(8):
            for near in range(4):
                row = k * 64 + near * 16
                for n in range(5):
                    at = near * TERM_ROWS + (first // CH + n) * 16
                    terms_out[k][at : at + 16, :] = block[row : row + 16, n * CH : (n + 1) * CH]


def nodes_kernel(rot, scaled, grad_dst, edge_rows, node_out, grad_local, back, terms):
    def turn(step, carry):
        e0 = pl.multiple_of(step * BLOCK, BLOCK)
        rows_here = pl.ds(e0, BLOCK)
        rotors = rot[rows_here, :].astype(F32)
        for degree, rows in ROWS_OF.items():
            first = degree * degree
            sums = [None] * (2 * degree + 1)
            for row in rows:
                a = scaled[rows_here, row * CH : (row + 1) * CH].astype(F32)
                b = grad_dst[rows_here, row * CH : (row + 1) * CH].astype(F32)
                for n in range(2 * degree + 1):
                    at = row * LCOEF + first + n
                    r = jnp.broadcast_to(rotors[:, at : at + 1], (BLOCK, CH))
                    sums[n] = (r * a, r * b) if sums[n] is None else (sums[n][0] + r * a, sums[n][1] + r * b)
            for n in range(2 * degree + 1):
                cut = slice((first + n) * CH, (first + n + 1) * CH)
                back[rows_here, cut] = sums[n][0].astype(BF16)
                terms[rows_here, cut] = sums[n][1].astype(BF16)
        return carry

    lax.fori_loop(0, EDGES // BLOCK, turn, 0)
    chosen = hot(edge_rows[1:2, :], (16, EDGES), 0)
    for first in range(0, FULL, 640):
        cut = slice(first, first + 640)
        node_out[:, cut] = mm(chosen, back[:, cut])[:4].astype(BF16)
        grad_local[:, cut] = mm(chosen, terms[:, cut])[:4]


def call(kernel, name, args, outs, scratch, flops, transcendentals=0):
    moved = sum(a.size * a.dtype.itemsize for a in args)
    return pl.pallas_call(
        kernel,
        out_shape=tuple(jax.ShapeDtypeStruct(s, t) for s, t in outs),
        in_specs=[pl.BlockSpec(memory_space=pltpu.VMEM)] * len(args),
        out_specs=tuple(pl.BlockSpec(memory_space=pltpu.VMEM) for _ in outs),
        scratch_shapes=[pltpu.VMEM(s, t) for s, t in scratch],
        compiler_params=pltpu.CompilerParams(vmem_limit_bytes=VMEM_LIMIT),
        cost_estimate=pl.CostEstimate(flops=flops, bytes_accessed=moved, transcendentals=transcendentals),
        name=name,
    )(*args)


def units_of(array):
    rows, width = array.shape
    return array.reshape(rows, width // CH, CH).transpose(1, 0, 2).reshape(-1, CH)


def index_maps(me):
    tables = []
    for rows in (10, 8, 6):
        k = np.arange(128 * rows)
        tables.append((k // rows, np.full_like(k, rows), k % rows))
    device, rows, rest = (jnp.asarray(np.concatenate(a), jnp.int32) for a in zip(*tables))
    near, far = device // 4, device % 4
    natural = block_owner(near, far, me) * rows + rest
    block, far = block_place(device, me)
    return jnp.concatenate([natural, (block * 4 + far) * rows + rest])[None]


def local(
    node_feat, rotation, source_owner, source_row, target_row, live_count, edge_bias,
    w_m0, w_m1, w_m2, w_alpha, out_grad,
):
    me = lax.axis_index("edge")
    features = node_feat[0]
    rotor_rows = rotation[0]
    live = (jnp.arange(EDGES, dtype=jnp.int32) < live_count[0, 0]).astype(jnp.int32)
    block, far = block_place(source_owner[0, :, 0], me)
    edge_rows = jnp.stack([block * 16 + far * 4 + source_row[0], target_row[0], live], axis=0)

    w1 = jnp.concatenate([w_m1[0], w_m1[1]], axis=1)
    w2 = jnp.concatenate([w_m2[0], w_m2[1]], axis=1)
    shards = (features, w_m0, w1, w2)
    own = jnp.concatenate([units_of(a) for a in shards], axis=0)
    blocks = [own] + [pull(own, dz=4 * a) for a in (1, 2, 3)]

    def merged(blocks, at, units, rows):
        parts = [b[at : at + units * rows].reshape(units, rows, CH) for b in blocks]
        return jnp.concatenate(parts, axis=1).reshape(-1, CH)

    far_parts, at = [], 0
    for shard in shards:
        rows, units = shard.shape[0], shard.shape[1] // CH
        far_parts.append(merged(blocks, at, units, rows))
        at += units * rows
    far_block = jnp.concatenate(far_parts, axis=0)
    blocks = [far_block] + [pull(far_block, dz=NEAR[n]) for n in (1, 2, 3)]
    feature_x = x_pieces(jnp.concatenate([b[:FAR_ROWS] for b in blocks], axis=0))
    near_parts, at = [], FAR_ROWS
    for units, depth in zip(UNITS, DEPTHS):
        near_parts.append(merged(blocks, at, units, depth))
        at += units * depth
    weight_x = x_pieces(jnp.concatenate(near_parts, axis=0))
    feature_pieces = feature_x + tuple(pull(a, dc=1) for a in feature_x)

    maps = index_maps(me)
    cotangent = out_grad[0]
    high = lax.reduce_precision(cotangent, 8, 7)
    own_rows = jnp.concatenate(
        [features, high.astype(BF16), (cotangent - high).astype(BF16), jnp.zeros((4, FULL), BF16)], axis=0
    )

    m0, m1, m2, turned_grad = call(
        rotate_kernel, "rotate",
        (*feature_pieces, rotor_rows, edge_rows, own_rows, maps),
        [((160, 1280), BF16), ((320, 1024), BF16), ((320, 768), BF16), ((160, MCOEF * CH), F32)],
        [((512, FULL), BF16), ((160, FULL), BF16), ((160, FULL), BF16), ((160, FULL), F32),
         ((160, 1280), BF16), ((320, 1024), BF16), ((320, 768), BF16)],
        3_000_000_000,
    )
    others = [lax.optimization_barrier((m0, weight_x[x]))[1] for x in (1, 2, 3)]
    weight_x = (weight_x[0], *others)
    weight_pieces = weight_x + tuple(pull(a, dc=1) for a in weight_x)
    outs = call(
        layer_kernel, "layer",
        (*weight_pieces, m0, m1, m2, turned_grad, rotor_rows, edge_bias[0].T, w_alpha.T, edge_rows, maps),
        [((4 * TERM_ROWS, CH), BF16)] * 8 + [((160, MCOEF * CH), BF16), ((160, MCOEF * CH), BF16)],
        [((1280, 640), BF16), ((1024, 1024), BF16), ((768, 768), BF16), ((160, MCOEF * CH), BF16),
         ((160, 640), BF16), ((320, 1024), BF16), ((320, 768), BF16),
         ((160, 1280), BF16), ((320, 1024), BF16), ((320, 768), BF16),
         ((160, 1280), BF16), ((320, 1024), BF16), ((320, 768), BF16), ((160, FULL), BF16)],
        5_000_000_000, 160 * 136,
    )
    term_pieces, (scaled, grad_dst) = outs[:8], outs[8:]
    node_out, grad_local = call(
        nodes_kernel, "nodes", (rotor_rows, scaled, grad_dst, edge_rows),
        [((4, FULL), BF16), ((4, FULL), F32)], [((160, FULL), BF16), ((160, FULL), BF16)],
        600_000_000,
    )
    terms, shard, (node_out, grad_local) = scatter_sum(term_pieces, (node_out, grad_local))
    grad_remote = terms.transpose(1, 0, 2).reshape(4, FULL)
    shard = shard.transpose(1, 0, 2).reshape(10, 640)
    n_rep = lax.axis_size("rep")
    copies = lax.all_to_all(jnp.broadcast_to(shard, (n_rep, 10, 640)), "rep", split_axis=0, concat_axis=0, tiled=True)
    grad_w0 = jnp.sum(copies, axis=0)
    return node_out[None], (grad_local + grad_remote)[None], grad_w0


def solution(mesh):
    placed = (
        P("rep", "edge", None), P("rep", "edge", None), P("rep", "edge", None), P("rep", "edge"),
        P("rep", "edge"), P("rep", "edge"), P("rep", "edge", None), P("edge", None),
        P(None, "edge", None), P(None, "edge", None), P(), P("rep", "edge", None),
    )
    return jax.shard_map(
        local, mesh=mesh, in_specs=placed,
        out_specs=(P("rep", "edge", None), P("rep", "edge", None), P("edge", None)),
        check_vma=False,
    )
```

```python
import jax
import jax.numpy as jnp
import numpy as np
from jax import lax
from jax.experimental import pallas as pl
from jax.experimental.pallas import tpu as pltpu
from jax.sharding import PartitionSpec as P

LCOEF = 25
MCOEF = 19
CH = 128
HEADS = 8
EDGES = 160
BLOCK = 16
NZ, NX = 16, 4
FULL = LCOEF * CH
ROWS_OF = {0: (0,), 1: (1, 5, 9), 2: (2, 6, 10, 13, 16), 3: (3, 7, 11, 14, 17), 4: (4, 8, 12, 15, 18)}
NEAR = (0, 1, 2, -1)
FAR_ROWS = 400
DEPTHS = (40, 32, 24)
UNITS = (5, 8, 6)
TERM_ROWS = 400 + 240
SOURCE_AT, TARGET_AT, POSITION_AT = (0, 1280, 2304), (3072, 4352, 5376), (6144, 7424, 8448)
VMEM_LIMIT = 56 * 2**20
F32, BF16 = jnp.float32, jnp.bfloat16


def where_to(i, dz, dx, dc):
    z, x, c = i // 8, (i // 2) % 4, i % 2
    sign = 1 - 2 * c
    return ((z + sign * dz) % NZ) * 8 + ((x + dx) % NX) * 2 + (c + dc) % 2


def pull(a, dz=0, dx=0, dc=0):
    return lax.ppermute(a, "edge", [(where_to(i, dz, dx, dc), i) for i in range(128)])


def push(a, dz=0, dx=0, dc=0):
    return lax.ppermute(a, "edge", [(i, where_to(i, dz, dx, dc)) for i in range(128)])


def block_place(owner, me):
    sign = 1 - 2 * (owner % 2)
    jz = (sign * (owner // 8 - me // 8) + 1) % NZ
    xr = ((owner // 2) % 4 - (me // 2) % 4) % NX
    cr = (owner % 2 + me % 2) % 2
    near = (jz % 4 + 3) % 4
    return cr * 16 + xr * 4 + near, jz // 4


def block_owner(place, far, me):
    cr, xr, near = place // 16, (place // 4) % 4, place % 4
    sign = 1 - 2 * ((me + cr) % 2)
    offset = (near + 1) % 4 - 1
    z = (me // 8 + sign * (4 * far + offset)) % NZ
    x = ((me // 2) % 4 + xr) % NX
    return z * 8 + x * 2 + (me % 2 + cr) % 2


def x_pieces(block):
    return (block,) + tuple(pull(block, dx=x) for x in (1, 2, 3))


def scatter_sum(pieces, beside):
    def add(a, *more):
        total = a.astype(F32)
        for m in more:
            total = total + m.astype(F32)
        return total

    a = [add(pieces[x], push(pieces[4 + x], dc=1)).astype(BF16) for x in range(4)]
    arrived, beside = lax.optimization_barrier(([push(a[x], dx=x) for x in (2, 1, 3)], beside))
    total = add(a[0], *arrived).astype(BF16)
    parts = [total[n * TERM_ROWS : (n + 1) * TERM_ROWS] for n in range(4)]
    total = add(parts[0], *(push(parts[n], dz=NEAR[n]) for n in (1, 2, 3))).astype(BF16)
    terms, shard = total[:400].reshape(25, 16, CH), total[400:].reshape(5, 48, CH)

    def part(n):
        return jnp.concatenate(
            [terms[:, 4 * n : 4 * n + 4].reshape(100, CH), shard[:, 10 * n : 10 * n + 10].reshape(50, CH)], axis=0
        )

    total = add(part(0), *(push(part(n), dz=4 * n) for n in (1, 2, 3)))
    return total[:100].reshape(25, 4, CH), total[100:].reshape(5, 10, CH), beside


def hot(index, shape, axis):
    return jnp.where(index == lax.broadcasted_iota(jnp.int32, shape, axis), F32(1), F32(0)).astype(BF16)


def mm(a, b):
    return jnp.dot(a, b, preferred_element_type=F32)


def mm_nt(a, b):
    return lax.dot_general(a, b, (((1,), (1,)), ((), ())), preferred_element_type=F32)


def mm_tn(a, b, precision=None):
    return lax.dot_general(a, b, (((0,), (0,)), ((), ())), precision=precision, preferred_element_type=F32)


def frame_slot(row):
    if row < 5:
        return 0, 0, row
    if row < 13:
        return 1, ((row - 5) // 4) * EDGES, (row - 5) % 4
    return 2, ((row - 13) // 3) * EDGES, (row - 13) % 3


def into_frames(rot, loads, stores):
    def turn(step, carry):
        e0 = pl.multiple_of(step * BLOCK, BLOCK)
        rows_here = pl.ds(e0, BLOCK)
        rotors = rot[rows_here, :].astype(F32)
        for degree, rows in ROWS_OF.items():
            sums = [None] * len(rows)
            for col in range(degree * degree, (degree + 1) ** 2):
                given = [load(rows_here, slice(col * CH, (col + 1) * CH)) for load in loads]
                for n, row in enumerate(rows):
                    r = jnp.broadcast_to(rotors[:, row * LCOEF + col : row * LCOEF + col + 1], (BLOCK, CH))
                    terms = [r * g for g in given]
                    sums[n] = terms if sums[n] is None else [a + b for a, b in zip(sums[n], terms)]
            for n, row in enumerate(rows):
                for store, total in zip(stores, sums[n]):
                    store(e0, row, total)
        return carry

    lax.fori_loop(0, EDGES // BLOCK, turn, 0)


def store_stacked(stacked):
    def store(e0, row, total):
        array, base, column = frame_slot(row)
        stacked[array][pl.ds(pl.multiple_of(base + e0, BLOCK), BLOCK), column * CH : (column + 1) * CH] = total.astype(BF16)

    return store


def local_kernel(rot, edge_rows, local, maps, m0, m1, m2, turned_grad, dstf, gradf, n0, n1, n2):
    t = edge_rows[1:2, :]
    rows = lax.broadcasted_iota(jnp.int32, (16, EDGES), 0)
    feat_hot = jnp.where(rows == t, F32(1), F32(0)).astype(BF16)
    grad_hot = jnp.where((rows == t + 4) | (rows == t + 8), F32(1), F32(0)).astype(BF16)
    for first in range(0, FULL, 640):
        cut = slice(first, first + 640)
        dstf[:, cut] = mm_tn(feat_hot, local[:, cut]).astype(BF16)
        gradf[:, cut] = mm_tn(grad_hot, local[:, cut])

    def store_grad(e0, row, total):
        turned_grad[pl.ds(e0, BLOCK), row * CH : (row + 1) * CH] = total

    into_frames(
        rot, [lambda rows, cut: dstf[rows, cut].astype(F32), lambda rows, cut: gradf[rows, cut]],
        [store_stacked((n0, n1, n2)), store_grad],
    )
    for natural, ordered, start in zip((n0, n1, n2), (m0, m1, m2), TARGET_AT):
        depth = natural.shape[1]
        for first in range(0, ordered.shape[1], 256):
            inverse = maps[:, start + first : start + first + 256]
            ordered[:, first : first + 256] = mm(natural[...], hot(inverse, (depth, 256), 0)).astype(BF16)


def layer_kernel(*refs):
    pieces = refs[:8]
    t0, t1, t2, turned_grad, rot, bias, alpha_ref, edge_rows, maps = refs[8:17]
    terms_out = refs[17:25]
    scaled_out, grad_dst = refs[25:27]
    w0, w1, w2, values, d0, d1, d2, p0, p1, p2, g0, g1, g2, src_terms, feats, n0, n1, n2, m0, m1, m2 = refs[27:]
    for k, piece in enumerate(pieces):
        for near in range(4):
            row = k * 64 + near * 16
            for u in range(LCOEF):
                at = near * FAR_ROWS + u * 16
                feats[row : row + 16, u * CH : (u + 1) * CH] = piece[at : at + 16, :]
        at = 4 * FAR_ROWS
        for out, units, depth in zip((w0, w1, w2), UNITS, DEPTHS):
            rows = 4 * depth
            for u in range(units):
                out[k * rows : (k + 1) * rows, u * CH : (u + 1) * CH] = piece[at : at + rows, :]
                at += rows
    source_hot = hot(edge_rows[0:1, :], (512, EDGES), 0)
    for first in range(0, FULL, 640):
        cut = slice(first, first + 640)
        src_terms[:, cut] = mm_tn(source_hot, feats[:, cut]).astype(BF16)
    into_frames(rot, [lambda rows, cut: src_terms[rows, cut].astype(F32)], [store_stacked((n0, n1, n2))])
    for natural, targets, ordered, start in zip((n0, n1, n2), (t0, t1, t2), (m0, m1, m2), SOURCE_AT):
        depth = natural.shape[1]
        for first in range(0, ordered.shape[1], 256):
            inverse = maps[:, start + first : start + first + 256]
            turned = mm(natural[...], hot(inverse, (depth, 256), 0))
            ordered[:, first : first + 256] = (turned + targets[:, first : first + 256].astype(F32)).astype(BF16)

    z0 = mm(m0[...], w0[...])
    for row in range(5):
        values[:, row * CH : (row + 1) * CH] = z0[:, row * CH : (row + 1) * CH].astype(BF16)
    z1 = mm(m1[...], w1[...])
    values[:, 5 * CH : 9 * CH] = (z1[:EDGES, :512] - z1[EDGES:, 512:]).astype(BF16)
    values[:, 9 * CH : 13 * CH] = (z1[EDGES:, :512] + z1[:EDGES, 512:]).astype(BF16)
    z2 = mm(m2[...], w2[...])
    values[:, 13 * CH : 16 * CH] = (z2[:EDGES, :384] - z2[EDGES:, 384:]).astype(BF16)
    values[:, 16 * CH : 19 * CH] = (z2[EDGES:, :384] + z2[:EDGES, 384:]).astype(BF16)

    v = z0[:, :CH]
    sigma = 1.0 / (1.0 + jnp.exp(-v))
    alpha = alpha_ref[...]
    logits = bias[...] + mm_nt(alpha, (v * sigma).astype(BF16))
    t = edge_rows[1:2, :]
    live = edge_rows[2:3, :] > 0
    members = [live & (t == n) for n in range(4)]

    def over_targets(array, empty, reduce):
        result = jnp.zeros((HEADS, EDGES), F32)
        for member in members:
            one = reduce(jnp.where(member, array, F32(empty)), axis=1, keepdims=True)
            result = jnp.where(member, one, result)
        return result

    top = over_targets(logits, -1e30, jnp.max)
    expo = jnp.where(live, jnp.exp(jnp.where(live, logits - top, F32(0))), F32(0))
    denom = jnp.where(live, over_targets(expo, 0.0, jnp.sum), F32(1))
    attn = expo / denom
    head_of = (
        lax.broadcasted_iota(jnp.int32, (HEADS, CH), 1) // (CH // HEADS)
        == lax.broadcasted_iota(jnp.int32, (HEADS, CH), 0)
    )
    spread = jnp.where(head_of, F32(1), F32(0))
    scale = mm_tn(attn, spread, lax.Precision.HIGHEST)
    dscale = jnp.zeros((EDGES, CH), F32)
    for row in range(MCOEF):
        cut = slice(row * CH, (row + 1) * CH)
        value = values[:, cut].astype(F32)
        dscale = dscale + turned_grad[:, cut] * value
        scaled_out[:, cut] = (scale * value).astype(BF16)
    dattn = lax.dot_general(
        spread, dscale, (((1,), (1,)), ((), ())), precision=lax.Precision.HIGHEST, preferred_element_type=F32
    )
    dlogits = attn * (dattn - over_targets(attn * dattn, 0.0, jnp.sum))
    dscalars = mm_tn(dlogits, alpha.astype(F32), lax.Precision.HIGHEST).astype(BF16).astype(F32)
    dv = dscalars * (sigma * (1.0 + v * (1.0 - sigma)))
    for row in range(MCOEF):
        cut = slice(row * CH, (row + 1) * CH)
        dvalue = (scale * turned_grad[:, cut]).astype(BF16)
        if row == 0:
            dvalue = (dvalue.astype(F32) + dv).astype(BF16)
        if row < 5:
            d0[:, cut] = dvalue
            continue
        out, width, column, plus = (d1, 512, (row - 5) % 4, row < 9) if row < 13 else (d2, 384, (row - 13) % 3, row < 16)
        a, b = column * CH, width + column * CH
        if plus:
            out[:EDGES, a : a + CH] = dvalue
            out[EDGES:, b : b + CH] = -dvalue
        else:
            out[EDGES:, a : a + CH] = dvalue
            out[:EDGES, b : b + CH] = dvalue
    dw = lax.dot_general(m0[...], d0[...], (((0,), (0,)), ((), ())), preferred_element_type=F32)
    for k in range(8):
        for near in range(4):
            row = (k * 4 + near) * 40
            for u in range(5):
                at = near * TERM_ROWS + 400 + u * 48
                rows = jnp.concatenate([dw[row : row + 40, u * CH : (u + 1) * CH], jnp.zeros((8, CH), F32)], axis=0)
                terms_out[k][at : at + 48, :] = rows.astype(BF16)
    for d, w, p, g, start in zip((d0, d1, d2), (w0, w1, w2), (p0, p1, p2), (g0, g1, g2), POSITION_AT):
        p[...] = mm_nt(d[...], w[...]).astype(BF16)
        for first in range(0, g.shape[1], 256):
            position = maps[:, start + first : start + first + 256]
            g[:, first : first + 256] = mm(p[...], hot(position, (w.shape[0], 256), 0)).astype(BF16)
    stacked = (g0, g1, g2)
    for row in range(MCOEF):
        array, base, column = frame_slot(row)
        grad_dst[:, row * CH : (row + 1) * CH] = stacked[array][base : base + EDGES, column * 256 + CH : column * 256 + 256]

    def turn(step, carry):
        e0 = pl.multiple_of(step * BLOCK, BLOCK)
        rows_here = pl.ds(e0, BLOCK)
        rotors = rot[rows_here, :].astype(F32)
        for degree, rows in ROWS_OF.items():
            first = degree * degree
            sums = [None] * (2 * degree + 1)
            for row in rows:
                array, base, column = frame_slot(row)
                s = stacked[array][pl.ds(pl.multiple_of(base + e0, BLOCK), BLOCK), column * 256 : column * 256 + CH]
                s = s.astype(F32)
                for n in range(2 * degree + 1):
                    at = row * LCOEF + first + n
                    term = jnp.broadcast_to(rotors[:, at : at + 1], (BLOCK, CH)) * s
                    sums[n] = term if sums[n] is None else sums[n] + term
            for n in range(2 * degree + 1):
                src_terms[rows_here, (first + n) * CH : (first + n + 1) * CH] = sums[n].astype(BF16)
        return carry

    lax.fori_loop(0, EDGES // BLOCK, turn, 0)
    chosen = hot(edge_rows[0:1, :], (512, EDGES), 0)
    for first in range(0, FULL, 640):
        block = mm(chosen, src_terms[:, first : first + 640]).astype(BF16)
        for k in range(8):
            for near in range(4):
                row = k * 64 + near * 16
                for n in range(5):
                    at = near * TERM_ROWS + (first // CH + n) * 16
                    terms_out[k][at : at + 16, :] = block[row : row + 16, n * CH : (n + 1) * CH]


def nodes_kernel(rot, scaled, grad_dst, edge_rows, node_out, grad_local, back, terms):
    def turn(step, carry):
        e0 = pl.multiple_of(step * BLOCK, BLOCK)
        rows_here = pl.ds(e0, BLOCK)
        rotors = rot[rows_here, :].astype(F32)
        for degree, rows in ROWS_OF.items():
            first = degree * degree
            sums = [None] * (2 * degree + 1)
            for row in rows:
                a = scaled[rows_here, row * CH : (row + 1) * CH].astype(F32)
                b = grad_dst[rows_here, row * CH : (row + 1) * CH].astype(F32)
                for n in range(2 * degree + 1):
                    at = row * LCOEF + first + n
                    r = jnp.broadcast_to(rotors[:, at : at + 1], (BLOCK, CH))
                    sums[n] = (r * a, r * b) if sums[n] is None else (sums[n][0] + r * a, sums[n][1] + r * b)
            for n in range(2 * degree + 1):
                cut = slice((first + n) * CH, (first + n + 1) * CH)
                back[rows_here, cut] = sums[n][0].astype(BF16)
                terms[rows_here, cut] = sums[n][1].astype(BF16)
        return carry

    lax.fori_loop(0, EDGES // BLOCK, turn, 0)
    chosen = hot(edge_rows[1:2, :], (16, EDGES), 0)
    for first in range(0, FULL, 640):
        cut = slice(first, first + 640)
        node_out[:, cut] = mm(chosen, back[:, cut])[:4].astype(BF16)
        grad_local[:, cut] = mm(chosen, terms[:, cut])[:4]


def call(kernel, name, args, outs, scratch, flops, transcendentals=0):
    moved = sum(a.size * a.dtype.itemsize for a in args)
    return pl.pallas_call(
        kernel,
        out_shape=tuple(jax.ShapeDtypeStruct(s, t) for s, t in outs),
        in_specs=[pl.BlockSpec(memory_space=pltpu.VMEM)] * len(args),
        out_specs=tuple(pl.BlockSpec(memory_space=pltpu.VMEM) for _ in outs),
        scratch_shapes=[pltpu.VMEM(s, t) for s, t in scratch],
        compiler_params=pltpu.CompilerParams(vmem_limit_bytes=VMEM_LIMIT),
        cost_estimate=pl.CostEstimate(flops=flops, bytes_accessed=moved, transcendentals=transcendentals),
        name=name,
    )(*args)


def units_of(array):
    rows, width = array.shape
    return array.reshape(rows, width // CH, CH).transpose(1, 0, 2).reshape(-1, CH)


def index_maps(me):
    tables = []
    for rows in (10, 8, 6):
        k = np.arange(128 * rows)
        tables.append((k // rows, np.full_like(k, rows), k % rows))
    device, rows, rest = (jnp.asarray(np.concatenate(a), jnp.int32) for a in zip(*tables))
    near, far = device // 4, device % 4
    natural = block_owner(near, far, me) * rows + rest
    block, far = block_place(device, me)
    column, channel = natural // 256, natural % 256
    source = jnp.where(channel < CH, column * CH + channel, -1)
    target = jnp.where(channel < CH, -1, column * CH + channel - CH)
    return jnp.concatenate([source, target, (block * 4 + far) * rows + rest])[None]


def local(
    node_feat, rotation, source_owner, source_row, target_row, live_count, edge_bias,
    w_m0, w_m1, w_m2, w_alpha, out_grad,
):
    me = lax.axis_index("edge")
    features = node_feat[0]
    rotor_rows = rotation[0]
    live = (jnp.arange(EDGES, dtype=jnp.int32) < live_count[0, 0]).astype(jnp.int32)
    block, far = block_place(source_owner[0, :, 0], me)
    edge_rows = jnp.stack([block * 16 + far * 4 + source_row[0], target_row[0], live], axis=0)

    w1 = jnp.concatenate([w_m1[0], w_m1[1]], axis=1)
    w2 = jnp.concatenate([w_m2[0], w_m2[1]], axis=1)
    shards = (features, w_m0, w1, w2)
    own = jnp.concatenate([units_of(a) for a in shards], axis=0)
    blocks = [own] + [pull(own, dz=4 * a) for a in (1, 2, 3)]

    def merged(blocks, at, units, rows):
        parts = [b[at : at + units * rows].reshape(units, rows, CH) for b in blocks]
        return jnp.concatenate(parts, axis=1).reshape(-1, CH)

    far_parts, at = [], 0
    for shard in shards:
        rows, units = shard.shape[0], shard.shape[1] // CH
        far_parts.append(merged(blocks, at, units, rows))
        at += units * rows
    far_block = jnp.concatenate(far_parts, axis=0)
    blocks = [far_block] + [pull(far_block, dz=NEAR[n]) for n in (1, 2, 3)]
    near_parts, at = [], FAR_ROWS
    for units, depth in zip(UNITS, DEPTHS):
        near_parts.append(merged(blocks, at, units, depth))
        at += units * depth
    pieces = x_pieces(jnp.concatenate([b[:FAR_ROWS] for b in blocks] + near_parts, axis=0))

    maps = index_maps(me)
    cotangent = out_grad[0]
    high = lax.reduce_precision(cotangent, 8, 7)
    own_rows = jnp.concatenate(
        [features, high.astype(BF16), (cotangent - high).astype(BF16), jnp.zeros((4, FULL), BF16)], axis=0
    )

    *targets, turned_grad = call(
        local_kernel, "local", (rotor_rows, edge_rows, own_rows, maps),
        [((160, 1280), BF16), ((320, 1024), BF16), ((320, 768), BF16), ((160, MCOEF * CH), F32)],
        [((160, FULL), BF16), ((160, FULL), F32), ((160, 640), BF16), ((320, 512), BF16), ((320, 384), BF16)],
        1_500_000_000,
    )
    pieces = (pieces[0], *(lax.optimization_barrier((targets[0], pieces[x]))[1] for x in (1, 2, 3)))
    pieces = pieces + tuple(pull(a, dc=1) for a in pieces)
    outs = call(
        layer_kernel, "layer",
        (*pieces, *targets, turned_grad, rotor_rows, edge_bias[0].T, w_alpha.T, edge_rows, maps),
        [((4 * TERM_ROWS, CH), BF16)] * 8 + [((160, MCOEF * CH), BF16), ((160, MCOEF * CH), BF16)],
        [((1280, 640), BF16), ((1024, 1024), BF16), ((768, 768), BF16), ((160, MCOEF * CH), BF16),
         ((160, 640), BF16), ((320, 1024), BF16), ((320, 768), BF16),
         ((160, 1280), BF16), ((320, 1024), BF16), ((320, 768), BF16),
         ((160, 1280), BF16), ((320, 1024), BF16), ((320, 768), BF16), ((160, FULL), BF16),
         ((512, FULL), BF16), ((160, 640), BF16), ((320, 512), BF16), ((320, 384), BF16),
         ((160, 1280), BF16), ((320, 1024), BF16), ((320, 768), BF16)],
        6_000_000_000, 160 * 136,
    )
    term_pieces, (scaled, grad_dst) = outs[:8], outs[8:]
    node_out, grad_local = call(
        nodes_kernel, "nodes", (rotor_rows, scaled, grad_dst, edge_rows),
        [((4, FULL), BF16), ((4, FULL), F32)], [((160, FULL), BF16), ((160, FULL), BF16)],
        600_000_000,
    )
    terms, shard, (node_out, grad_local) = scatter_sum(term_pieces, (node_out, grad_local))
    grad_remote = terms.transpose(1, 0, 2).reshape(4, FULL)
    shard = shard.transpose(1, 0, 2).reshape(10, 640)
    n_rep = lax.axis_size("rep")
    copies = lax.all_to_all(jnp.broadcast_to(shard, (n_rep, 10, 640)), "rep", split_axis=0, concat_axis=0, tiled=True)
    grad_w0 = jnp.sum(copies, axis=0)
    return node_out[None], (grad_local + grad_remote)[None], grad_w0


def solution(mesh):
    placed = (
        P("rep", "edge", None), P("rep", "edge", None), P("rep", "edge", None), P("rep", "edge"),
        P("rep", "edge"), P("rep", "edge"), P("rep", "edge", None), P("edge", None),
        P(None, "edge", None), P(None, "edge", None), P(), P("rep", "edge", None),
    )
    return jax.shard_map(
        local, mesh=mesh, in_specs=placed,
        out_specs=(P("rep", "edge", None), P("rep", "edge", None), P("edge", None)),
        check_vma=False,
    )
```

```python
import jax
import jax.numpy as jnp
import numpy as np
from jax import lax
from jax.experimental import pallas as pl
from jax.experimental.pallas import tpu as pltpu
from jax.sharding import PartitionSpec as P

LCOEF = 25
MCOEF = 19
CH = 128
HEADS = 8
EDGES = 160
BLOCK = 16
NZ, NX = 16, 4
FULL = LCOEF * CH
ROWS_OF = {0: (0,), 1: (1, 5, 9), 2: (2, 6, 10, 13, 16), 3: (3, 7, 11, 14, 17), 4: (4, 8, 12, 15, 18)}
NEAR = (0, 1, 2, -1)
FAR_ROWS = 400
DEPTHS = (40, 32, 24)
UNITS = (5, 8, 6)
TERM_ROWS = 400 + 240
X_SPLIT = 1600 + 3 * 160
SOURCE_AT, TARGET_AT, POSITION_AT = (0, 1280, 2304), (3072, 4352, 5376), (6144, 7424, 8448)
VMEM_LIMIT = 56 * 2**20
F32, BF16 = jnp.float32, jnp.bfloat16


def where_to(i, dz, dx, dc):
    z, x, c = i // 8, (i // 2) % 4, i % 2
    sign = 1 - 2 * c
    return ((z + sign * dz) % NZ) * 8 + ((x + dx) % NX) * 2 + (c + dc) % 2


def pull(a, dz=0, dx=0, dc=0):
    return lax.ppermute(a, "edge", [(where_to(i, dz, dx, dc), i) for i in range(128)])


def push(a, dz=0, dx=0, dc=0):
    return lax.ppermute(a, "edge", [(i, where_to(i, dz, dx, dc)) for i in range(128)])


def block_place(owner, me):
    sign = 1 - 2 * (owner % 2)
    jz = (sign * (owner // 8 - me // 8) + 1) % NZ
    xr = ((owner // 2) % 4 - (me // 2) % 4) % NX
    cr = (owner % 2 + me % 2) % 2
    near = (jz % 4 + 3) % 4
    return cr * 16 + xr * 4 + near, jz // 4


def block_owner(place, far, me):
    cr, xr, near = place // 16, (place // 4) % 4, place % 4
    sign = 1 - 2 * ((me + cr) % 2)
    offset = (near + 1) % 4 - 1
    z = (me // 8 + sign * (4 * far + offset)) % NZ
    x = ((me // 2) % 4 + xr) % NX
    return z * 8 + x * 2 + (me % 2 + cr) % 2


def gather_x(block, first):
    right, left = pull(block, dx=1), pull(block, dx=3)
    right, left = (lax.optimization_barrier((first, a))[1] for a in (right, left))
    return block, right, pull(right[:X_SPLIT], dx=1), pull(left[X_SPLIT:], dx=3), left


def scatter_sum(pieces, beside):
    def add(a, *more):
        total = a.astype(F32)
        for m in more:
            total = total + m.astype(F32)
        return total

    a = [add(pieces[x], push(pieces[4 + x], dc=1)).astype(BF16) for x in range(4)]
    half = 2 * TERM_ROWS
    up, down = push(a[2][:half], dx=1), push(a[2][half:], dx=3)
    right = push(jnp.concatenate([add(a[1][:half], up).astype(BF16), a[1][half:]], axis=0), dx=1)
    left = push(jnp.concatenate([a[3][:half], add(a[3][half:], down).astype(BF16)], axis=0), dx=3)
    (right, left), beside = lax.optimization_barrier(((right, left), beside))
    total = add(a[0], right, left).astype(BF16)
    parts = [total[n * TERM_ROWS : (n + 1) * TERM_ROWS] for n in range(4)]
    total = add(parts[0], *(push(parts[n], dz=NEAR[n]) for n in (1, 2, 3))).astype(BF16)
    terms, shard = total[:400].reshape(25, 16, CH), total[400:].reshape(5, 48, CH)

    def part(n):
        return jnp.concatenate(
            [terms[:, 4 * n : 4 * n + 4].reshape(100, CH), shard[:, 10 * n : 10 * n + 10].reshape(50, CH)], axis=0
        )

    total = add(part(0), *(push(part(n), dz=4 * n) for n in (1, 2, 3)))
    return total[:100].reshape(25, 4, CH), total[100:].reshape(5, 10, CH), beside


def hot(index, shape, axis):
    return jnp.where(index == lax.broadcasted_iota(jnp.int32, shape, axis), F32(1), F32(0)).astype(BF16)


def mm(a, b):
    return jnp.dot(a, b, preferred_element_type=F32)


def mm_nt(a, b):
    return lax.dot_general(a, b, (((1,), (1,)), ((), ())), preferred_element_type=F32)


def mm_tn(a, b, precision=None):
    return lax.dot_general(a, b, (((0,), (0,)), ((), ())), precision=precision, preferred_element_type=F32)


def frame_slot(row):
    if row < 5:
        return 0, 0, row
    if row < 13:
        return 1, ((row - 5) // 4) * EDGES, (row - 5) % 4
    return 2, ((row - 13) // 3) * EDGES, (row - 13) % 3


def into_frames(rot, loads, stores):
    def turn(step, carry):
        e0 = pl.multiple_of(step * BLOCK, BLOCK)
        rows_here = pl.ds(e0, BLOCK)
        rotors = rot[rows_here, :].astype(F32)
        for degree, rows in ROWS_OF.items():
            sums = [None] * len(rows)
            for col in range(degree * degree, (degree + 1) ** 2):
                given = [load(rows_here, slice(col * CH, (col + 1) * CH)) for load in loads]
                for n, row in enumerate(rows):
                    r = jnp.broadcast_to(rotors[:, row * LCOEF + col : row * LCOEF + col + 1], (BLOCK, CH))
                    terms = [r * g for g in given]
                    sums[n] = terms if sums[n] is None else [a + b for a, b in zip(sums[n], terms)]
            for n, row in enumerate(rows):
                for store, total in zip(stores, sums[n]):
                    store(e0, row, total)
        return carry

    lax.fori_loop(0, EDGES // BLOCK, turn, 0)


def store_stacked(stacked):
    def store(e0, row, total):
        array, base, column = frame_slot(row)
        stacked[array][pl.ds(pl.multiple_of(base + e0, BLOCK), BLOCK), column * CH : (column + 1) * CH] = total.astype(BF16)

    return store


def local_kernel(rot, edge_rows, local, maps, m0, m1, m2, turned_grad, dstf, gradf, n0, n1, n2):
    t = edge_rows[1:2, :]
    rows = lax.broadcasted_iota(jnp.int32, (16, EDGES), 0)
    feat_hot = jnp.where(rows == t, F32(1), F32(0)).astype(BF16)
    grad_hot = jnp.where((rows == t + 4) | (rows == t + 8), F32(1), F32(0)).astype(BF16)
    for first in range(0, FULL, 640):
        cut = slice(first, first + 640)
        dstf[:, cut] = mm_tn(feat_hot, local[:, cut]).astype(BF16)
        gradf[:, cut] = mm_tn(grad_hot, local[:, cut])

    def store_grad(e0, row, total):
        turned_grad[pl.ds(e0, BLOCK), row * CH : (row + 1) * CH] = total

    into_frames(
        rot, [lambda rows, cut: dstf[rows, cut].astype(F32), lambda rows, cut: gradf[rows, cut]],
        [store_stacked((n0, n1, n2)), store_grad],
    )
    for natural, ordered, start in zip((n0, n1, n2), (m0, m1, m2), TARGET_AT):
        depth = natural.shape[1]
        for first in range(0, ordered.shape[1], 256):
            inverse = maps[:, start + first : start + first + 256]
            ordered[:, first : first + 256] = mm(natural[...], hot(inverse, (depth, 256), 0)).astype(BF16)


def layer_kernel(*refs):
    t0, t1, t2, turned_grad, rot, bias, alpha_ref, edge_rows, maps = refs[10:19]
    terms_out = refs[19:27]
    scaled_out, grad_dst = refs[27:29]
    w0, w1, w2, values, d0, d1, d2, p0, p1, p2, g0, g1, g2, src_terms, feats, n0, n1, n2, m0, m1, m2 = refs[29:]
    for k in range(8):
        own, right, upper, lower, left = refs[k // 4 * 5 : k // 4 * 5 + 5]

        def rows_at(at, rows, whole=(own, right, None, left)[k % 4], upper=upper, lower=lower):
            if whole is not None:
                return whole[at : at + rows, :]
            return upper[at : at + rows, :] if at < X_SPLIT else lower[at - X_SPLIT : at - X_SPLIT + rows, :]

        for near in range(4):
            row = k * 64 + near * 16
            for u in range(LCOEF):
                feats[row : row + 16, u * CH : (u + 1) * CH] = rows_at(near * FAR_ROWS + u * 16, 16)
        at = 4 * FAR_ROWS
        for out, units, depth in zip((w0, w1, w2), UNITS, DEPTHS):
            rows = 4 * depth
            for u in range(units):
                out[k * rows : (k + 1) * rows, u * CH : (u + 1) * CH] = rows_at(at, rows)
                at += rows
    source_hot = hot(edge_rows[0:1, :], (512, EDGES), 0)
    for first in range(0, FULL, 640):
        cut = slice(first, first + 640)
        src_terms[:, cut] = mm_tn(source_hot, feats[:, cut]).astype(BF16)
    into_frames(rot, [lambda rows, cut: src_terms[rows, cut].astype(F32)], [store_stacked((n0, n1, n2))])
    for natural, targets, ordered, start in zip((n0, n1, n2), (t0, t1, t2), (m0, m1, m2), SOURCE_AT):
        depth = natural.shape[1]
        for first in range(0, ordered.shape[1], 256):
            inverse = maps[:, start + first : start + first + 256]
            turned = mm(natural[...], hot(inverse, (depth, 256), 0))
            ordered[:, first : first + 256] = (turned + targets[:, first : first + 256].astype(F32)).astype(BF16)

    z0 = mm(m0[...], w0[...])
    for row in range(5):
        values[:, row * CH : (row + 1) * CH] = z0[:, row * CH : (row + 1) * CH].astype(BF16)
    z1 = mm(m1[...], w1[...])
    values[:, 5 * CH : 9 * CH] = (z1[:EDGES, :512] - z1[EDGES:, 512:]).astype(BF16)
    values[:, 9 * CH : 13 * CH] = (z1[EDGES:, :512] + z1[:EDGES, 512:]).astype(BF16)
    z2 = mm(m2[...], w2[...])
    values[:, 13 * CH : 16 * CH] = (z2[:EDGES, :384] - z2[EDGES:, 384:]).astype(BF16)
    values[:, 16 * CH : 19 * CH] = (z2[EDGES:, :384] + z2[:EDGES, 384:]).astype(BF16)

    v = z0[:, :CH]
    sigma = 1.0 / (1.0 + jnp.exp(-v))
    alpha = alpha_ref[...]
    logits = bias[...] + mm_nt(alpha, (v * sigma).astype(BF16))
    t = edge_rows[1:2, :]
    live = edge_rows[2:3, :] > 0
    members = [live & (t == n) for n in range(4)]

    def over_targets(array, empty, reduce):
        result = jnp.zeros((HEADS, EDGES), F32)
        for member in members:
            one = reduce(jnp.where(member, array, F32(empty)), axis=1, keepdims=True)
            result = jnp.where(member, one, result)
        return result

    top = over_targets(logits, -1e30, jnp.max)
    expo = jnp.where(live, jnp.exp(jnp.where(live, logits - top, F32(0))), F32(0))
    denom = jnp.where(live, over_targets(expo, 0.0, jnp.sum), F32(1))
    attn = expo / denom
    head_of = (
        lax.broadcasted_iota(jnp.int32, (HEADS, CH), 1) // (CH // HEADS)
        == lax.broadcasted_iota(jnp.int32, (HEADS, CH), 0)
    )
    spread = jnp.where(head_of, F32(1), F32(0))
    scale = mm_tn(attn, spread, lax.Precision.HIGHEST)
    dscale = jnp.zeros((EDGES, CH), F32)
    for row in range(MCOEF):
        cut = slice(row * CH, (row + 1) * CH)
        value = values[:, cut].astype(F32)
        dscale = dscale + turned_grad[:, cut] * value
        scaled_out[:, cut] = (scale * value).astype(BF16)
    dattn = lax.dot_general(
        spread, dscale, (((1,), (1,)), ((), ())), precision=lax.Precision.HIGHEST, preferred_element_type=F32
    )
    dlogits = attn * (dattn - over_targets(attn * dattn, 0.0, jnp.sum))
    dscalars = mm_tn(dlogits, alpha.astype(F32), lax.Precision.HIGHEST).astype(BF16).astype(F32)
    dv = dscalars * (sigma * (1.0 + v * (1.0 - sigma)))
    for row in range(MCOEF):
        cut = slice(row * CH, (row + 1) * CH)
        dvalue = (scale * turned_grad[:, cut]).astype(BF16)
        if row == 0:
            dvalue = (dvalue.astype(F32) + dv).astype(BF16)
        if row < 5:
            d0[:, cut] = dvalue
            continue
        out, width, column, plus = (d1, 512, (row - 5) % 4, row < 9) if row < 13 else (d2, 384, (row - 13) % 3, row < 16)
        a, b = column * CH, width + column * CH
        if plus:
            out[:EDGES, a : a + CH] = dvalue
            out[EDGES:, b : b + CH] = -dvalue
        else:
            out[EDGES:, a : a + CH] = dvalue
            out[:EDGES, b : b + CH] = dvalue
    dw = lax.dot_general(m0[...], d0[...], (((0,), (0,)), ((), ())), preferred_element_type=F32)
    for k in range(8):
        for near in range(4):
            row = (k * 4 + near) * 40
            for u in range(5):
                at = near * TERM_ROWS + 400 + u * 48
                rows = jnp.concatenate([dw[row : row + 40, u * CH : (u + 1) * CH], jnp.zeros((8, CH), F32)], axis=0)
                terms_out[k][at : at + 48, :] = rows.astype(BF16)
    for d, w, p, g, start in zip((d0, d1, d2), (w0, w1, w2), (p0, p1, p2), (g0, g1, g2), POSITION_AT):
        p[...] = mm_nt(d[...], w[...]).astype(BF16)
        for first in range(0, g.shape[1], 256):
            position = maps[:, start + first : start + first + 256]
            g[:, first : first + 256] = mm(p[...], hot(position, (w.shape[0], 256), 0)).astype(BF16)
    stacked = (g0, g1, g2)
    for row in range(MCOEF):
        array, base, column = frame_slot(row)
        grad_dst[:, row * CH : (row + 1) * CH] = stacked[array][base : base + EDGES, column * 256 + CH : column * 256 + 256]

    def turn(step, carry):
        e0 = pl.multiple_of(step * BLOCK, BLOCK)
        rows_here = pl.ds(e0, BLOCK)
        rotors = rot[rows_here, :].astype(F32)
        for degree, rows in ROWS_OF.items():
            first = degree * degree
            sums = [None] * (2 * degree + 1)
            for row in rows:
                array, base, column = frame_slot(row)
                s = stacked[array][pl.ds(pl.multiple_of(base + e0, BLOCK), BLOCK), column * 256 : column * 256 + CH]
                s = s.astype(F32)
                for n in range(2 * degree + 1):
                    at = row * LCOEF + first + n
                    term = jnp.broadcast_to(rotors[:, at : at + 1], (BLOCK, CH)) * s
                    sums[n] = term if sums[n] is None else sums[n] + term
            for n in range(2 * degree + 1):
                src_terms[rows_here, (first + n) * CH : (first + n + 1) * CH] = sums[n].astype(BF16)
        return carry

    lax.fori_loop(0, EDGES // BLOCK, turn, 0)
    chosen = hot(edge_rows[0:1, :], (512, EDGES), 0)
    for first in range(0, FULL, 640):
        block = mm(chosen, src_terms[:, first : first + 640]).astype(BF16)
        for k in range(8):
            for near in range(4):
                row = k * 64 + near * 16
                for n in range(5):
                    at = near * TERM_ROWS + (first // CH + n) * 16
                    terms_out[k][at : at + 16, :] = block[row : row + 16, n * CH : (n + 1) * CH]


def nodes_kernel(rot, scaled, grad_dst, edge_rows, node_out, grad_local, back, terms):
    def turn(step, carry):
        e0 = pl.multiple_of(step * BLOCK, BLOCK)
        rows_here = pl.ds(e0, BLOCK)
        rotors = rot[rows_here, :].astype(F32)
        for degree, rows in ROWS_OF.items():
            first = degree * degree
            sums = [None] * (2 * degree + 1)
            for row in rows:
                a = scaled[rows_here, row * CH : (row + 1) * CH].astype(F32)
                b = grad_dst[rows_here, row * CH : (row + 1) * CH].astype(F32)
                for n in range(2 * degree + 1):
                    at = row * LCOEF + first + n
                    r = jnp.broadcast_to(rotors[:, at : at + 1], (BLOCK, CH))
                    sums[n] = (r * a, r * b) if sums[n] is None else (sums[n][0] + r * a, sums[n][1] + r * b)
            for n in range(2 * degree + 1):
                cut = slice((first + n) * CH, (first + n + 1) * CH)
                back[rows_here, cut] = sums[n][0].astype(BF16)
                terms[rows_here, cut] = sums[n][1].astype(BF16)
        return carry

    lax.fori_loop(0, EDGES // BLOCK, turn, 0)
    chosen = hot(edge_rows[1:2, :], (16, EDGES), 0)
    for first in range(0, FULL, 640):
        cut = slice(first, first + 640)
        node_out[:, cut] = mm(chosen, back[:, cut])[:4].astype(BF16)
        grad_local[:, cut] = mm(chosen, terms[:, cut])[:4]


def call(kernel, name, args, outs, scratch, flops, transcendentals=0):
    moved = sum(a.size * a.dtype.itemsize for a in args)
    return pl.pallas_call(
        kernel,
        out_shape=tuple(jax.ShapeDtypeStruct(s, t) for s, t in outs),
        in_specs=[pl.BlockSpec(memory_space=pltpu.VMEM)] * len(args),
        out_specs=tuple(pl.BlockSpec(memory_space=pltpu.VMEM) for _ in outs),
        scratch_shapes=[pltpu.VMEM(s, t) for s, t in scratch],
        compiler_params=pltpu.CompilerParams(vmem_limit_bytes=VMEM_LIMIT),
        cost_estimate=pl.CostEstimate(flops=flops, bytes_accessed=moved, transcendentals=transcendentals),
        name=name,
    )(*args)


def units_of(array):
    rows, width = array.shape
    return array.reshape(rows, width // CH, CH).transpose(1, 0, 2).reshape(-1, CH)


def index_maps(me):
    tables = []
    for rows in (10, 8, 6):
        k = np.arange(128 * rows)
        tables.append((k // rows, np.full_like(k, rows), k % rows))
    device, rows, rest = (jnp.asarray(np.concatenate(a), jnp.int32) for a in zip(*tables))
    near, far = device // 4, device % 4
    natural = block_owner(near, far, me) * rows + rest
    block, far = block_place(device, me)
    column, channel = natural // 256, natural % 256
    source = jnp.where(channel < CH, column * CH + channel, -1)
    target = jnp.where(channel < CH, -1, column * CH + channel - CH)
    return jnp.concatenate([source, target, (block * 4 + far) * rows + rest])[None]


def local(
    node_feat, rotation, source_owner, source_row, target_row, live_count, edge_bias,
    w_m0, w_m1, w_m2, w_alpha, out_grad,
):
    me = lax.axis_index("edge")
    features = node_feat[0]
    rotor_rows = rotation[0]
    live = (jnp.arange(EDGES, dtype=jnp.int32) < live_count[0, 0]).astype(jnp.int32)
    block, far = block_place(source_owner[0, :, 0], me)
    edge_rows = jnp.stack([block * 16 + far * 4 + source_row[0], target_row[0], live], axis=0)

    w1 = jnp.concatenate([w_m1[0], w_m1[1]], axis=1)
    w2 = jnp.concatenate([w_m2[0], w_m2[1]], axis=1)
    shards = (features, w_m0, w1, w2)
    own = jnp.concatenate([units_of(a) for a in shards], axis=0)
    blocks = [own] + [pull(own, dz=4 * a) for a in (1, 2, 3)]

    def merged(blocks, at, units, rows):
        parts = [b[at : at + units * rows].reshape(units, rows, CH) for b in blocks]
        return jnp.concatenate(parts, axis=1).reshape(-1, CH)

    far_parts, at = [], 0
    for shard in shards:
        rows, units = shard.shape[0], shard.shape[1] // CH
        far_parts.append(merged(blocks, at, units, rows))
        at += units * rows
    far_block = jnp.concatenate(far_parts, axis=0)
    blocks = [far_block] + [pull(far_block, dz=NEAR[n]) for n in (1, 2, 3)]
    near_parts, at = [], FAR_ROWS
    for units, depth in zip(UNITS, DEPTHS):
        near_parts.append(merged(blocks, at, units, depth))
        at += units * depth
    near_block = jnp.concatenate([b[:FAR_ROWS] for b in blocks] + near_parts, axis=0)

    maps = index_maps(me)
    cotangent = out_grad[0]
    high = lax.reduce_precision(cotangent, 8, 7)
    own_rows = jnp.concatenate(
        [features, high.astype(BF16), (cotangent - high).astype(BF16), jnp.zeros((4, FULL), BF16)], axis=0
    )

    *targets, turned_grad = call(
        local_kernel, "local", (rotor_rows, edge_rows, own_rows, maps),
        [((160, 1280), BF16), ((320, 1024), BF16), ((320, 768), BF16), ((160, MCOEF * CH), F32)],
        [((160, FULL), BF16), ((160, FULL), F32), ((160, 640), BF16), ((320, 512), BF16), ((320, 384), BF16)],
        1_500_000_000,
    )
    pieces = gather_x(near_block, targets[0])
    pieces = pieces + tuple(pull(a, dc=1) for a in pieces)
    outs = call(
        layer_kernel, "layer",
        (*pieces, *targets, turned_grad, rotor_rows, edge_bias[0].T, w_alpha.T, edge_rows, maps),
        [((4 * TERM_ROWS, CH), BF16)] * 8 + [((160, MCOEF * CH), BF16), ((160, MCOEF * CH), BF16)],
        [((1280, 640), BF16), ((1024, 1024), BF16), ((768, 768), BF16), ((160, MCOEF * CH), BF16),
         ((160, 640), BF16), ((320, 1024), BF16), ((320, 768), BF16),
         ((160, 1280), BF16), ((320, 1024), BF16), ((320, 768), BF16),
         ((160, 1280), BF16), ((320, 1024), BF16), ((320, 768), BF16), ((160, FULL), BF16),
         ((512, FULL), BF16), ((160, 640), BF16), ((320, 512), BF16), ((320, 384), BF16),
         ((160, 1280), BF16), ((320, 1024), BF16), ((320, 768), BF16)],
        6_000_000_000, 160 * 136,
    )
    term_pieces, (scaled, grad_dst) = outs[:8], outs[8:]
    node_out, grad_local = call(
        nodes_kernel, "nodes", (rotor_rows, scaled, grad_dst, edge_rows),
        [((4, FULL), BF16), ((4, FULL), F32)], [((160, FULL), BF16), ((160, FULL), BF16)],
        600_000_000,
    )
    terms, shard, (node_out, grad_local) = scatter_sum(term_pieces, (node_out, grad_local))
    grad_remote = terms.transpose(1, 0, 2).reshape(4, FULL)
    shard = shard.transpose(1, 0, 2).reshape(10, 640)
    n_rep = lax.axis_size("rep")
    copies = lax.all_to_all(jnp.broadcast_to(shard, (n_rep, 10, 640)), "rep", split_axis=0, concat_axis=0, tiled=True)
    grad_w0 = jnp.sum(copies, axis=0)
    return node_out[None], (grad_local + grad_remote)[None], grad_w0


def solution(mesh):
    placed = (
        P("rep", "edge", None), P("rep", "edge", None), P("rep", "edge", None), P("rep", "edge"),
        P("rep", "edge"), P("rep", "edge"), P("rep", "edge", None), P("edge", None),
        P(None, "edge", None), P(None, "edge", None), P(), P("rep", "edge", None),
    )
    return jax.shard_map(
        local, mesh=mesh, in_specs=placed,
        out_specs=(P("rep", "edge", None), P("rep", "edge", None), P("edge", None)),
        check_vma=False,
    )
```
